32 devices in a mesh: img: 8 (over z, y), blk: 4 (over x, core).
Axes of the slice: x: 2, y: 2, z: 4, core: 2. Of those that a mesh axis runs over, the one named last changes fastest.
Arguments:
- tokens: bfloat16 [32, 256, 4, 384], P('img', None, 'blk'), may hold values from -6 to 6
- lengths: int32 [32, 10], P('img'), may hold values from 0 to 325, as said below
- keep_in: int32 [32, 256, 4], P('img', None, 'blk'), may hold values 0 or 1
- noise: float32 [32, 256, 4, 2], P('img', None, 'blk'), may hold values from -2.5 to 8
- first_gain: float32 [384], replicated, may hold values from 0.5 to 1.5
- first_shift: float32 [384], replicated, may hold values from -1.25 to 1.25
- qkv_weight: bfloat16 [384, 1152], replicated, may hold values from -0.3125 to 0.3125
- proj_weight: bfloat16 [384, 384], replicated, may hold values from -2.5 to 2.5
- proj_bias: float32 [384], replicated, may hold values from -1.25 to 1.25
- second_gain: float32 [384], replicated, may hold values from 0.5 to 1.5
- second_shift: float32 [384], replicated, may hold values from -1.25 to 1.25
- expand_weight: bfloat16 [384, 1536], replicated, may hold values from -0.3125 to 0.3125
- expand_bias: float32 [1536], replicated, may hold values from -1.25 to 1.25
- reduce_weight: bfloat16 [1536, 384], replicated, may hold values from -0.15625 to 0.15625
- reduce_bias: float32 [384], replicated, may hold values from -2.5 to 2.5
- score_gain: float32 [384], replicated, may hold values from 0.5 to 1.5
- score_shift: float32 [384], replicated, may hold values from -1.25 to 1.25
- score_weight: bfloat16 [384, 384], replicated, may hold values from -0.3125 to 0.3125
- score_bias: float32 [384], replicated, may hold values from -1.25 to 1.25
- pred_weight: bfloat16 [384, 192], replicated, may hold values from -0.3125 to 0.3125
- pred_bias: float32 [192], replicated, may hold values from -1.25 to 1.25
- mid_weight: bfloat16 [192, 96], replicated, may hold values from -0.4375 to 0.4375
- mid_bias: float32 [96], replicated, may hold values from -1.25 to 1.25
- last_weight: bfloat16 [96, 2], replicated, may hold values from -0.625 to 0.625
- last_bias: float32 [2], replicated, may hold values from -1.25 to 1.25
- grad_out: bfloat16 [32, 256, 4, 384], P('img', None, 'blk'), may hold values from -6 to 6
- grad_keep: float32 [32, 256, 4], P('img', None, 'blk'), may hold values from -6 to 6
Outputs:
- out_tokens: bfloat16 [32, 256, 4, 384], P('img', None, 'blk')
- keep_prob: float32 [32, 256, 4], P('img', None, 'blk')
- tokens_grad: bfloat16 [32, 256, 4, 384], P('img', None, 'blk')
- first_gain_grad: float32 [384], replicated
- first_shift_grad: float32 [384], replicated
- qkv_weight_grad: float32 [384, 1152], replicated
- proj_weight_grad: float32 [384, 384], replicated
- proj_bias_grad: float32 [384], replicated
- second_gain_grad: float32 [384], replicated
- second_shift_grad: float32 [384], replicated
- expand_weight_grad: float32 [384, 1536], replicated
- expand_bias_grad: float32 [1536], replicated
- reduce_weight_grad: float32 [1536, 384], replicated
- reduce_bias_grad: float32 [384], replicated
- score_gain_grad: float32 [384], replicated
- score_shift_grad: float32 [384], replicated
- score_weight_grad: float32 [384, 384], replicated
- score_bias_grad: float32 [384], replicated
- pred_weight_grad: float32 [384, 192], replicated
- pred_bias_grad: float32 [192], replicated
- mid_weight_grad: float32 [192, 96], replicated
- mid_bias_grad: float32 [96], replicated
- last_weight_grad: float32 [96, 2], replicated
- last_bias_grad: float32 [2], replicated
The draws below stay inside these ranges and needn't reach their ends.
Inputs may be any that keep to these rules, and one draw needn't show every extreme that they name: `lengths`: per slot: the images' token counts in order. The first is 325; each other is one of 101, 197, 325 (for slots under 650 tokens these scaled by 1024 / 650, at least 4) or 0 once the slot is full; they sum to at most 1024, the rest of the slot is padding.
All inputs are finite; a program needn't handle non-finite values. No bound on the sum of `keep_in` on one device may be relied on, other than what follows from the above.
Results may differ from the reference program's by a relative error of at most 0.035.
Values may be sent and summed in bfloat16 or wider, within the bound.
A program may use at most 256 MiB of HBM per device.

```python
import jax
import jax.numpy as jnp
from jax import lax

D = 384
HEADS = 6
HEAD = 64
FF = 1536
PRED = 192
MID = 96
TOK_DEV = 256
SLOTS = 32
IMGS = 10
N_BLK = 4


def draw_lengths(key, part):
    key = jax.random.fold_in(key, 11)
    slot_len = TOK_DEV * N_BLK
    if slot_len >= 650:
        options = jnp.array([101, 197, 325], jnp.int32)
        largest = 325
    else:
        options = jnp.array([max(N_BLK, 101 * slot_len // 650), max(N_BLK, 197 * slot_len // 650), max(N_BLK, 325 * slot_len // 650)], jnp.int32)
        largest = max(N_BLK, 325 * slot_len // 650)
    picks = jax.random.randint(key, (SLOTS, IMGS), 0, 3)
    choose = jnp.sum(jnp.where(picks[..., None] == jnp.arange(3)[None, None, :], options[None, None, :], 0), -1)
    choose = jnp.where(jnp.arange(IMGS)[None, :] == 0, largest, choose)
    image_ends = jnp.cumsum(choose, 1)
    return jnp.where(image_ends <= slot_len, choose, 0).astype(jnp.int32)


def draw_noise(key, part):
    key = jax.random.fold_in(key, 12)
    sample = jax.random.gumbel(key, (SLOTS, TOK_DEV, N_BLK, 2), jnp.float32)
    return jnp.clip(sample, -2.5, 8.0)


def place_ends(drawn, stream_key, smallest, top_value):
    shape = drawn.shape
    spot = [jax.random.randint(jax.random.fold_in(stream_key, axis), (), 0, shape[axis]) for axis in range(len(shape))]
    drawn = drawn.at[tuple(spot)].set(smallest)
    longest = shape.index(max(shape))
    spot[longest] = (spot[longest] + 1) % shape[longest]
    return drawn.at[tuple(spot)].set(top_value)


def steps_of(own_key, dims, shards, low, top_value):
    def one(axis_at, shards_of):
        draws = jax.random.uniform(jax.random.fold_in(jax.random.fold_in(own_key, 6), axis_at), (shards_of,), jnp.float32, low / len(shards), top_value / len(shards))
        return jnp.repeat(jnp.exp(draws), dims[axis_at] // shards_of).reshape((-1,) + (1,) * (len(dims) - axis_at - 1))

    gain = one(*shards[0])
    for cut in shards[1:]:
        gain = gain * one(*cut)
    return gain


def gaussian(stream_key, extent, scale, most, cuts=(), kind=jnp.bfloat16):
    result = jax.random.normal(stream_key, extent, jnp.float32) * scale
    if len(cuts) > 0:
        result = steps_of(stream_key, extent, cuts, -0.22, 0.18) * result
    return jnp.clip(result, min=-most, max=most).astype(kind)


def setup_inputs(seed: int = 0) -> dict:
    arg_keys = jax.random.split(jax.random.key(seed), 28)
    return {
        "tokens": gaussian(arg_keys[0], (SLOTS, TOK_DEV, N_BLK, D), 1.0, 6.0, ((0, 8), (2, 4))),
        "lengths": draw_lengths(jax.random.fold_in(arg_keys[27], 71), 0),
        "keep_in": place_ends((jax.random.randint(arg_keys[2], (SLOTS, TOK_DEV, N_BLK), 0, 10) < 7).astype(jnp.int32), jax.random.fold_in(arg_keys[2], 1), 0, 1),
        "noise": draw_noise(jax.random.fold_in(arg_keys[27], 71), 0),
        "first_gain": jnp.clip(1.0 + 0.1 * jax.random.normal(arg_keys[4], (D,), jnp.float32), 0.5, 1.5),
        "first_shift": gaussian(arg_keys[5], (D,), 0.2, 1.25, (), jnp.float32),
        "qkv_weight": gaussian(arg_keys[6], (D, 3 * D), D ** -0.5, 0.3125),
        "proj_weight": gaussian(arg_keys[7], (D, D), (D // 64) ** -0.5, 2.5),
        "proj_bias": gaussian(arg_keys[8], (D,), 0.2, 1.25, (), jnp.float32),
        "second_gain": jnp.clip(1.0 + 0.1 * jax.random.normal(arg_keys[9], (D,), jnp.float32), 0.5, 1.5),
        "second_shift": gaussian(arg_keys[10], (D,), 0.2, 1.25, (), jnp.float32),
        "expand_weight": gaussian(arg_keys[11], (D, FF), D ** -0.5, 0.3125),
        "expand_bias": gaussian(arg_keys[12], (FF,), 0.2, 1.25, (), jnp.float32),
        "reduce_weight": gaussian(arg_keys[13], (FF, D), FF ** -0.5, 0.15625),
        "reduce_bias": gaussian(arg_keys[14], (D,), 0.4, 2.5, (), jnp.float32),
        "score_gain": jnp.clip(1.0 + 0.1 * jax.random.normal(arg_keys[15], (D,), jnp.float32), 0.5, 1.5),
        "score_shift": gaussian(arg_keys[16], (D,), 0.2, 1.25, (), jnp.float32),
        "score_weight": gaussian(arg_keys[17], (D, D), D ** -0.5, 0.3125),
        "score_bias": gaussian(arg_keys[18], (D,), 0.2, 1.25, (), jnp.float32),
        "pred_weight": gaussian(arg_keys[19], (D, PRED), D ** -0.5, 0.3125),
        "pred_bias": gaussian(arg_keys[20], (PRED,), 0.2, 1.25, (), jnp.float32),
        "mid_weight": gaussian(arg_keys[21], (PRED, MID), PRED ** -0.5, 0.4375),
        "mid_bias": gaussian(arg_keys[22], (MID,), 0.2, 1.25, (), jnp.float32),
        "last_weight": gaussian(arg_keys[23], (MID, 2), MID ** -0.5, 0.625),
        "last_bias": gaussian(arg_keys[24], (2,), 0.2, 1.25, (), jnp.float32),
        "grad_out": gaussian(arg_keys[25], (SLOTS, TOK_DEV, N_BLK, D), 1.0, 6.0, ((0, 8), (2, 4))),
        "grad_keep": gaussian(arg_keys[26], (SLOTS, TOK_DEV, N_BLK), 1.0, 6.0, ((0, 8), (2, 4)), jnp.float32),
    }


EPS = 1e-06
NEG = -1e+30
HIGH = lax.Precision.HIGHEST

@jax.custom_vjp
def low(v):
    return lax.optimization_barrier(v.astype(jnp.bfloat16)).astype(jnp.float32)

@jax.custom_vjp
def low_back(v):
    return v

def low_keep(v):
    return (low(v), None)

def low_pass(kept, grad):
    return (grad,)

def back_keep(v):
    return (v, None)

def back_low(kept, grad):
    return (low(grad),)
low.defvjp(low_keep, low_pass)
low_back.defvjp(back_keep, back_low)

def layer_norm(row_data, norm_gain, norm_shift):
    centre = row_data - lax.optimization_barrier(jnp.mean(row_data, -1, keepdims=True))
    spread = lax.optimization_barrier(jnp.mean(centre * centre, -1, keepdims=True))
    return centre * lax.rsqrt(spread + EPS) * norm_gain + norm_shift

def gelu_exact(values):
    return jax.nn.gelu(values, approximate=False)

def dense(former, latter):
    return jnp.dot(former, latter, precision=HIGH, preferred_element_type=jnp.float32)

def slot_forward(weights, row_data, keep_row, noise_row, slot_lengths):
    first_gain, first_shift, qkv_weight, proj_weight, proj_bias, second_gain, second_shift, expand_weight, expand_bias, reduce_weight, reduce_bias, score_gain, score_shift, score_weight, score_bias, pred_weight, pred_bias, mid_weight, mid_bias, last_weight, last_bias = weights
    length = row_data.shape[0]
    model_width = row_data.shape[1]
    places = jnp.arange(length, dtype=jnp.int32)
    image_ends = jnp.cumsum(slot_lengths)
    segment = lax.optimization_barrier(jnp.sum((image_ends[None, :] <= places[:, None]).astype(jnp.int32), 1))
    live_mask = places < image_ends[-1]
    kept_mask = (keep_row > 0) & live_mask
    allowed = (segment[:, None] == segment[None, :]) & kept_mask[None, :] | (places[:, None] == places[None, :])
    normed = low(layer_norm(row_data, first_gain, first_shift))
    qkv_rows = low_back(dense(normed, qkv_weight))
    query_rows = low(qkv_rows[:, :model_width] * 0.125).reshape(length, HEADS, HEAD)
    key_rows = low(qkv_rows[:, model_width:2 * model_width]).reshape(length, HEADS, HEAD)
    value_rows = low(qkv_rows[:, 2 * model_width:]).reshape(length, HEADS, HEAD)
    scores = low_back(jnp.einsum('qhd,khd->hqk', query_rows, key_rows, precision=HIGH))
    scores = jnp.where(allowed[None], scores, NEG)
    shifted = scores - lax.optimization_barrier(jnp.max(scores, -1, keepdims=True))
    expos = jnp.where(allowed[None], jnp.exp(shifted), 0.0)
    probs = expos / lax.optimization_barrier(jnp.sum(expos, -1, keepdims=True))
    attended = jnp.einsum('hqk,khd->qhd', low(probs), value_rows, precision=HIGH).reshape(length, model_width)
    attended = low(low_back(attended))
    hidden = row_data + low_back(dense(attended, proj_weight) + proj_bias)
    normed_two = low(layer_norm(hidden, second_gain, second_shift))
    expand = low_back(dense(normed_two, expand_weight) + expand_bias)
    active = low(gelu_exact(expand))
    block = hidden + low_back(dense(active, reduce_weight) + reduce_bias)
    out_rows = block * live_mask.astype(jnp.float32)[:, None]
    score_in = low(layer_norm(block, score_gain, score_shift))
    score_pre = low_back(dense(score_in, score_weight) + score_bias)
    score_act = gelu_exact(score_pre)
    half_width = score_act.shape[1] // 2
    image_count = slot_lengths.shape[0]
    member = (segment[:, None] == jnp.arange(image_count, dtype=jnp.int32)[None, :]).astype(jnp.float32)
    chosen = member * kept_mask.astype(jnp.float32)[:, None]
    image_sums = jnp.dot(chosen.T, score_act[:, half_width:], precision=HIGH)
    image_counts = lax.optimization_barrier(jnp.sum(chosen, 0))
    image_means = image_sums / jnp.maximum(image_counts, 1.0)[:, None]
    spread_mean = jnp.dot(member, image_means, precision=HIGH)
    joined = low(jnp.concatenate([score_act[:, :half_width], spread_mean], 1))
    pred_pre = low_back(dense(joined, pred_weight) + pred_bias)
    pred_act = low(gelu_exact(pred_pre))
    mid_pre = low_back(dense(pred_act, mid_weight) + mid_bias)
    mid_act = low(gelu_exact(mid_pre))
    logits = dense(mid_act, last_weight) + last_bias
    margin = logits[:, 0] - logits[:, 1] + noise_row[:, 0] - noise_row[:, 1]
    keep_share = jax.nn.sigmoid(margin) * kept_mask.astype(jnp.float32)
    return (out_rows, keep_share)

def reference(tokens, lengths, keep_in, noise, first_gain, first_shift, qkv_weight, proj_weight, proj_bias, second_gain, second_shift, expand_weight, expand_bias, reduce_weight, reduce_bias, score_gain, score_shift, score_weight, score_bias, pred_weight, pred_bias, mid_weight, mid_bias, last_weight, last_bias, grad_out, grad_keep):
    slot_count, per_slot, axis_count, model_width = tokens.shape
    length = per_slot * axis_count
    row_data = tokens.astype(jnp.float32).reshape(slot_count, length, model_width)
    keep_rows = keep_in.reshape(slot_count, length)
    noise_rows = noise.reshape(slot_count, length, 2)
    weights = tuple((item.astype(jnp.float32) for item in (first_gain, first_shift, qkv_weight, proj_weight, proj_bias, second_gain, second_shift, expand_weight, expand_bias, reduce_weight, reduce_bias, score_gain, score_shift, score_weight, score_bias, pred_weight, pred_bias, mid_weight, mid_bias, last_weight, last_bias)))

    def forward(rows_all, weight_all):

        def one_slot(slot_items):
            return slot_forward(weight_all, slot_items[0], slot_items[1], slot_items[2], slot_items[3])
        return lax.map(jax.checkpoint(one_slot), (rows_all, keep_rows, noise_rows, lengths))
    (out_rows, keep_share), pull = jax.vjp(forward, row_data, weights)
    row_grad, weight_grads = pull((grad_out.astype(jnp.float32).reshape(slot_count, length, model_width), grad_keep.reshape(slot_count, length)))
    return (out_rows.reshape(tokens.shape).astype(jnp.bfloat16), keep_share.reshape(keep_in.shape), row_grad.reshape(tokens.shape).astype(jnp.bfloat16), weight_grads[0], weight_grads[1], weight_grads[2], weight_grads[3], weight_grads[4], weight_grads[5], weight_grads[6], weight_grads[7], weight_grads[8], weight_grads[9], weight_grads[10], weight_grads[11], weight_grads[12], weight_grads[13], weight_grads[14], weight_grads[15], weight_grads[16], weight_grads[17], weight_grads[18], weight_grads[19], weight_grads[20])
```

```python
import functools
import math
from types import SimpleNamespace

import jax
import jax.numpy as jnp
from jax import lax
from jax.experimental import pallas as pl
from jax.experimental.pallas import tpu as pltpu
from jax.sharding import PartitionSpec as P

HEAD = 64

EPS = 1e-06
NEG = -1e30
HIGH = lax.Precision.HIGHEST


def layer_norm(row_data, norm_gain, norm_shift):
    centre = row_data - jnp.mean(row_data, -1, keepdims=True)
    spread = jnp.mean(centre * centre, -1, keepdims=True)
    return centre * lax.rsqrt(spread + EPS) * norm_gain + norm_shift


def gelu_exact(values):
    return jax.nn.gelu(values, approximate=False)


def matmul(former, latter):
    return jnp.dot(former, latter, preferred_element_type=jnp.float32)


def left_outer(former, latter):
    return lax.dot_general(
        former, latter, (((0,), (0,)), ((), ())), preferred_element_type=jnp.float32
    )


def right_outer(former, latter):
    return lax.dot_general(
        former, latter, (((1,), (1,)), ((), ())), preferred_element_type=jnp.float32
    )


def column_sum(values):
    return jnp.sum(values.astype(jnp.float32), 0)


def general_device(
    tokens,
    lengths,
    keep_in,
    noise,
    first_gain,
    first_shift,
    qkv_weight,
    proj_weight,
    proj_bias,
    second_gain,
    second_shift,
    expand_weight,
    expand_bias,
    reduce_weight,
    reduce_bias,
    score_gain,
    score_shift,
    score_weight,
    score_bias,
    pred_weight,
    pred_bias,
    mid_weight,
    mid_bias,
    last_weight,
    last_bias,
    grad_out,
    grad_keep,
):
    slot_count, per_slot, _, model_width = tokens.shape
    row_count = slot_count * per_slot
    head_count = model_width // HEAD
    axis_count = lax.axis_size("blk")
    axis_place = lax.axis_index("blk")
    image_ends = jnp.cumsum(lengths, 1)
    totals = image_ends[:, -1:]
    image_count = lengths.shape[1]

    def locate(places):
        segment = jnp.sum((image_ends[:, None, :] <= places[None, :, None]).astype(jnp.int32), -1)
        return (segment, places[None, :] < totals)

    query_place = jnp.arange(per_slot, dtype=jnp.int32) * axis_count + axis_place
    query_segment, query_live = locate(query_place)
    kept_mask = (keep_in[:, :, 0] > 0) & query_live
    kept_float = kept_mask.astype(jnp.float32)
    live_float = query_live.astype(jnp.float32).reshape(row_count, 1)
    kept_rows = kept_float.reshape(row_count)
    row_data = tokens.reshape(row_count, model_width).astype(jnp.float32)
    normed, first_back = jax.vjp(layer_norm, row_data, first_gain, first_shift)
    normed_low = normed.astype(jnp.bfloat16)
    qkv_rows = matmul(normed_low, qkv_weight)
    query_low = (
        (qkv_rows[:, :model_width] * 0.125)
        .astype(jnp.bfloat16)
        .reshape(slot_count, per_slot, head_count, HEAD)
    )
    key_value = (
        qkv_rows[:, model_width:]
        .astype(jnp.bfloat16)
        .reshape(slot_count, per_slot, 1, 2 * model_width)
    )
    keep_send = keep_in.astype(jnp.bfloat16)

    def scores_for(pieces):
        key_piece, keep_piece = pieces
        piece_width = key_piece.shape[2]
        key_place = (
            jnp.arange(per_slot, dtype=jnp.int32)[:, None] * axis_count
            + jnp.arange(piece_width, dtype=jnp.int32)[None, :]
        ).reshape(per_slot * piece_width)
        key_segment, key_live = locate(key_place)
        key_kept = (keep_piece.reshape(slot_count, per_slot * piece_width) > 0) & key_live
        allowed = (query_segment[:, :, None] == key_segment[:, None, :]) & key_kept[:, None, :] | (
            query_place[:, None] == key_place[None, :]
        )[None]
        split_keys = key_piece.reshape(slot_count, per_slot * piece_width, 2, head_count, HEAD)
        key_rows = split_keys[:, :, 0]
        value_rows = split_keys[:, :, 1]
        scores = jnp.einsum(
            "sqhd,skhd->shqk", query_low, key_rows, preferred_element_type=jnp.float32
        )
        return (scores, allowed[:, None], key_rows, value_rows)

    run_max = jnp.full((slot_count, head_count, per_slot), NEG, jnp.float32)
    summed = jnp.zeros((slot_count, per_slot, head_count, HEAD), jnp.float32)
    scores, allowed, key_rows, value_rows = scores_for(
        (
            lax.all_gather(key_value, "blk", axis=2, tiled=True),
            lax.all_gather(keep_send, "blk", axis=2, tiled=True),
        )
    )
    scores = jnp.where(allowed, scores, NEG)
    new_max = jnp.maximum(run_max, jnp.max(scores, -1))
    weights = jnp.where(allowed, jnp.exp(scores - new_max[..., None]), 0.0)
    factor = jnp.exp(run_max - new_max)
    update = jnp.einsum(
        "shqk,skhd->sqhd",
        weights.astype(jnp.bfloat16),
        value_rows,
        preferred_element_type=jnp.float32,
    )
    summed = summed * jnp.swapaxes(factor, 1, 2)[..., None] + update
    run_max, run_sum, summed = (new_max, jnp.sum(weights, -1), summed)
    out_heads = summed / jnp.swapaxes(run_sum, 1, 2)[..., None]
    log_total = run_max + jnp.log(run_sum)
    attended_low = out_heads.reshape(row_count, model_width).astype(jnp.bfloat16)
    hidden = row_data + matmul(attended_low, proj_weight) + proj_bias
    normed_two, second_back = jax.vjp(layer_norm, hidden, second_gain, second_shift)
    normed_two_low = normed_two.astype(jnp.bfloat16)
    expand = matmul(normed_two_low, expand_weight) + expand_bias
    active, expand_back = jax.vjp(gelu_exact, expand)
    active_low = active.astype(jnp.bfloat16)
    block = hidden + matmul(active_low, reduce_weight) + reduce_bias
    out_tokens = (block * live_float).astype(jnp.bfloat16).reshape(tokens.shape)
    score_in, score_back = jax.vjp(layer_norm, block, score_gain, score_shift)
    score_low = score_in.astype(jnp.bfloat16)
    score_pre = matmul(score_low, score_weight) + score_bias
    score_act, score_gelu_back = jax.vjp(gelu_exact, score_pre)
    half_width = score_act.shape[1] // 2
    member = (
        query_segment[:, :, None] == jnp.arange(image_count, dtype=jnp.int32)[None, None, :]
    ).astype(jnp.float32)
    chosen = member * kept_float[..., None]
    global_part = score_act[:, half_width:].reshape(slot_count, per_slot, half_width)
    part_sums = jnp.einsum("sti,stc->sic", chosen, global_part, precision=HIGH)
    part_counts = jnp.sum(chosen, 1)
    image_sums, image_counts = (
        lax.psum(part_sums.astype(jnp.bfloat16), "blk").astype(jnp.float32),
        lax.psum(part_counts.astype(jnp.bfloat16), "blk").astype(jnp.float32),
    )
    inverse = 1.0 / jnp.maximum(image_counts, 1.0)
    image_means = image_sums * inverse[..., None]
    spread_mean = jnp.einsum("sti,sic->stc", member, image_means, precision=HIGH).reshape(
        row_count, half_width
    )
    joined_low = jnp.concatenate([score_act[:, :half_width], spread_mean], 1).astype(jnp.bfloat16)
    pred_pre = matmul(joined_low, pred_weight) + pred_bias
    pred_act, pred_gelu_back = jax.vjp(gelu_exact, pred_pre)
    pred_low = pred_act.astype(jnp.bfloat16)
    mid_pre = matmul(pred_low, mid_weight) + mid_bias
    mid_act, mid_gelu_back = jax.vjp(gelu_exact, mid_pre)
    mid_low = mid_act.astype(jnp.bfloat16)
    logits = matmul(mid_low, last_weight) + last_bias
    noise_rows = noise.reshape(row_count, 2)
    margin = logits[:, 0] - logits[:, 1] + noise_rows[:, 0] - noise_rows[:, 1]
    keep_sigmoid = jax.nn.sigmoid(margin)
    keep_prob = (keep_sigmoid * kept_rows).reshape(keep_in.shape)
    margin_grad = grad_keep.reshape(row_count) * kept_rows * keep_sigmoid * (1.0 - keep_sigmoid)
    logit_grad = jnp.stack([margin_grad, -margin_grad], 1)
    last_weight_grad = lax.dot_general(
        mid_low.astype(jnp.float32), logit_grad, (((0,), (0,)), ((), ())), precision=HIGH
    )
    last_bias_grad = jnp.sum(logit_grad, 0)
    mid_grad = lax.dot_general(
        logit_grad, last_weight.astype(jnp.float32), (((1,), (1,)), ((), ())), precision=HIGH
    )
    mid_pre_low = mid_gelu_back(mid_grad)[0].astype(jnp.bfloat16)
    mid_weight_grad = left_outer(pred_low, mid_pre_low)
    mid_bias_grad = column_sum(mid_pre_low)
    pred_pre_low = pred_gelu_back(right_outer(mid_pre_low, mid_weight))[0].astype(jnp.bfloat16)
    pred_weight_grad = left_outer(joined_low, pred_pre_low)
    pred_bias_grad = column_sum(pred_pre_low)
    joined_grad = right_outer(pred_pre_low, pred_weight)
    spread_grad = joined_grad[:, half_width:].reshape(slot_count, per_slot, half_width)
    part_mean_grad = jnp.einsum("sti,stc->sic", member, spread_grad, precision=HIGH)
    mean_grad = lax.psum(part_mean_grad.astype(jnp.bfloat16), "blk").astype(jnp.float32)
    global_grad = jnp.einsum(
        "sti,sic->stc", chosen, mean_grad * inverse[..., None], precision=HIGH
    ).reshape(row_count, half_width)
    act_grad = jnp.concatenate([joined_grad[:, :half_width], global_grad], 1)
    score_pre_low = score_gelu_back(act_grad)[0].astype(jnp.bfloat16)
    score_weight_grad = left_outer(score_low, score_pre_low)
    score_bias_grad = column_sum(score_pre_low)
    block_pred_grad, score_gain_grad, score_shift_grad = score_back(
        right_outer(score_pre_low, score_weight)
    )
    block_grad = (
        block_pred_grad + grad_out.reshape(row_count, model_width).astype(jnp.float32) * live_float
    )
    block_low = block_grad.astype(jnp.bfloat16)
    reduce_weight_grad = left_outer(active_low, block_low)
    reduce_bias_grad = column_sum(block_low)
    expand_low = expand_back(right_outer(block_low, reduce_weight))[0].astype(jnp.bfloat16)
    expand_weight_grad = left_outer(normed_two_low, expand_low)
    expand_bias_grad = column_sum(expand_low)
    hidden_ln_grad, second_gain_grad, second_shift_grad = second_back(
        right_outer(expand_low, expand_weight)
    )
    hidden_grad = hidden_ln_grad + block_grad
    hidden_low = hidden_grad.astype(jnp.bfloat16)
    proj_weight_grad = left_outer(attended_low, hidden_low)
    proj_bias_grad = column_sum(hidden_low)
    out_grad_low = (
        right_outer(hidden_low, proj_weight)
        .astype(jnp.bfloat16)
        .reshape(slot_count, per_slot, head_count, HEAD)
    )
    row_delta = jnp.einsum("sqhd,sqhd->shq", out_grad_low.astype(jnp.float32), out_heads)
    pieces = (
        lax.all_gather(key_value, "blk", axis=2, tiled=True),
        lax.all_gather(keep_send, "blk", axis=2, tiled=True),
    )
    scores, allowed, key_rows, value_rows = scores_for(pieces)
    piece_width = pieces[0].shape[2]
    probs = jnp.where(allowed, jnp.exp(scores - log_total[..., None]), 0.0)
    prob_grad = jnp.einsum(
        "sqhd,skhd->shqk", out_grad_low, value_rows, preferred_element_type=jnp.float32
    )
    score_grad = (probs * (prob_grad - row_delta[..., None])).astype(jnp.bfloat16)
    query_grad = jnp.einsum(
        "shqk,skhd->sqhd", score_grad, key_rows, preferred_element_type=jnp.float32
    )
    key_grad = jnp.einsum(
        "shqk,sqhd->skhd", score_grad, query_low, preferred_element_type=jnp.float32
    )
    value_grad = jnp.einsum(
        "shqk,sqhd->skhd",
        probs.astype(jnp.bfloat16),
        out_grad_low,
        preferred_element_type=jnp.float32,
    )
    piece_grad = jnp.stack([key_grad, value_grad], 2).reshape(
        slot_count, per_slot, piece_width, 2 * model_width
    )
    pair_grad = piece_grad
    query_grad, pair_grad = (query_grad, pair_grad)
    own_pair = (
        lax.psum_scatter(pair_grad.astype(jnp.bfloat16), "blk", scatter_dimension=2, tiled=True)
        .astype(jnp.float32)
        .reshape(row_count, 2 * model_width)
    )
    qkv_low = jnp.concatenate(
        [query_grad.reshape(row_count, model_width) * 0.125, own_pair], 1
    ).astype(jnp.bfloat16)
    qkv_weight_grad = left_outer(normed_low, qkv_low)
    input_grad, first_gain_grad, first_shift_grad = first_back(right_outer(qkv_low, qkv_weight))
    tokens_grad = (input_grad + hidden_grad).astype(jnp.bfloat16).reshape(tokens.shape)
    (
        first_gain_grad,
        first_shift_grad,
        qkv_weight_grad,
        proj_weight_grad,
        proj_bias_grad,
        second_gain_grad,
        second_shift_grad,
        expand_weight_grad,
        expand_bias_grad,
        reduce_weight_grad,
        reduce_bias_grad,
        score_gain_grad,
        score_shift_grad,
        score_weight_grad,
        score_bias_grad,
        pred_weight_grad,
        pred_bias_grad,
        mid_weight_grad,
        mid_bias_grad,
        last_weight_grad,
        last_bias_grad,
    ) = lax.psum(
        (
            first_gain_grad,
            first_shift_grad,
            qkv_weight_grad,
            proj_weight_grad,
            proj_bias_grad,
            second_gain_grad,
            second_shift_grad,
            expand_weight_grad,
            expand_bias_grad,
            reduce_weight_grad,
            reduce_bias_grad,
            score_gain_grad,
            score_shift_grad,
            score_weight_grad,
            score_bias_grad,
            pred_weight_grad,
            pred_bias_grad,
            mid_weight_grad,
            mid_bias_grad,
            last_weight_grad,
            last_bias_grad,
        ),
        ("img", "blk"),
    )
    return (
        out_tokens,
        keep_prob,
        tokens_grad,
        first_gain_grad,
        first_shift_grad,
        qkv_weight_grad,
        proj_weight_grad,
        proj_bias_grad,
        second_gain_grad,
        second_shift_grad,
        expand_weight_grad,
        expand_bias_grad,
        reduce_weight_grad,
        reduce_bias_grad,
        score_gain_grad,
        score_shift_grad,
        score_weight_grad,
        score_bias_grad,
        pred_weight_grad,
        pred_bias_grad,
        mid_weight_grad,
        mid_bias_grad,
        last_weight_grad,
        last_bias_grad,
    )


LONGEST = 325
CHUNK = 32
ROWS = 256
BF = jnp.bfloat16
F32 = jnp.float32


def dot(a, b):
    return lax.dot_general(a, b, (((1,), (0,)), ((), ())), preferred_element_type=F32)


def dot_nt(a, b):
    return lax.dot_general(a, b, (((1,), (1,)), ((), ())), preferred_element_type=F32)


def dot_tn(a, b):
    return lax.dot_general(a, b, (((0,), (0,)), ((), ())), preferred_element_type=F32)


def split_two(v):
    high = v.astype(BF)
    return high, (v - high.astype(F32)).astype(BF)


def gelu_pair(v):
    phi = 0.5 * (1.0 + lax.erf(v * math.sqrt(0.5)))
    density = jnp.exp(v * v * -0.5) * (1.0 / math.sqrt(2.0 * math.pi))
    return v * phi, phi + v * density


def normalise(v):
    centre = v - jnp.mean(v, -1, keepdims=True)
    spread = jnp.mean(centre * centre, -1, keepdims=True)
    scale = lax.rsqrt(spread + EPS)
    return centre * scale, scale


def norm_back(grad, unit, scale, gain):
    inner = grad * gain
    mean_one = jnp.mean(inner, -1, keepdims=True)
    mean_two = jnp.mean(inner * unit, -1, keepdims=True)
    return scale * (inner - mean_one - unit * mean_two)


def total_rows(v):
    return jnp.sum(v.astype(F32), 0, keepdims=True)


def lanes(width):
    return lax.broadcasted_iota(jnp.int32, (1, width), 1)


def features(v):
    high = v.astype(BF)
    rest = v - high.astype(F32)
    middle = rest.astype(BF)
    least = (rest - middle.astype(F32)).astype(BF)
    spot = lanes(v.shape[1]) % HEAD
    zero = jnp.zeros_like(high)
    return jnp.where(spot == 0, high, jnp.where(spot == 1, middle, jnp.where(spot == 2, least, zero)))


def window(first, last, length, tile):
    if length < 650:
        return 0, length
    low = 0 if first < LONGEST else max(LONGEST, first - LONGEST + 1)
    high = LONGEST if last <= LONGEST else min(length, last - 1 + LONGEST)
    return low // tile * tile, min(length, -(-high // tile) * tile)


class Place:
    def __init__(self, axis, length, ends):
        self.axis, self.length, self.ends = axis, length, ends
        self.tile = CHUNK * axis

    def places(self, rows):
        return rows // self.tile * self.tile + rows % CHUNK * self.axis + rows % self.tile // CHUNK

    def segments(self, places):
        total = jnp.zeros_like(places)
        for end in self.ends:
            total += (places >= end).astype(jnp.int32)
        return total

    def column(self, start, count):
        rows = start + lax.broadcasted_iota(jnp.int32, (count, 1), 0)
        return self.places(rows)

    def row(self, start, count):
        rows = start + lax.broadcasted_iota(jnp.int32, (1, count), 1)
        return self.places(rows)


VEC = SimpleNamespace(
    first_gain=0, first_shift=1, proj_bias=2, second_gain=3, second_shift=4, expand_bias=5, reduce_bias=9,
    score_gain=10, score_shift=11, score_bias=12, pred_bias=13, mid_bias=14, last_weight=15, last_bias=16,
)
VEC_ROWS = 32
MESH = pl.DeviceIdType.MESH
VMEM = pltpu.VMEM
DMA = pltpu.SemaphoreType.DMA


def names_of(**named):
    return tuple(named)


WEIGHTS = names_of(
    first_gain=0, first_shift=0, qkv_weight=0, proj_weight=0, proj_bias=0, second_gain=0, second_shift=0,
    expand_weight=0, expand_bias=0, reduce_weight=0, reduce_bias=0, score_gain=0, score_shift=0, score_weight=0,
    score_bias=0, pred_weight=0, pred_bias=0, mid_weight=0, mid_bias=0, last_weight=0, last_bias=0,
)
LARGE = names_of(
    qkv_weight=0, proj_weight=0, expand_weight=0, reduce_weight=0, score_weight=0, pred_weight=0, mid_weight=0
)
LAST_BIAS = WEIGHTS[-1]
LOADED = LARGE + tuple(n for n in WEIGHTS if n not in LARGE and n != LAST_BIAS)
SUMS = 7


class Sizes:
    def __init__(self, axis, groups, width, model, hidden, mid, images):
        self.axis, self.groups, self.width, self.model = axis, groups, width, model
        self.hidden, self.mid, self.images = hidden, mid, images
        self.length = axis * width
        self.tile = CHUNK * axis
        self.tiles = self.length // self.tile
        self.pairs = model // 128
        self.far = groups // 2
        step = 8 * self.far * 16
        self.filled = [0] * SUMS
        wide = model * self.pairs
        self.at = SimpleNamespace(
            score=self.reserve(0, wide), pred=self.reserve(0, model // 2 * self.pairs), mid=self.reserve(0, model // 2),
            reduce=self.reserve(1, hidden * self.pairs), expand=self.reserve(2, model * (hidden // 128)),
            proj=self.reserve(3, wide),
            qkv=[self.reserve(3 + min(p, 2), 3 * model) for p in range(self.pairs)],
            vec=self.reserve(6, VEC_ROWS * self.pairs),
        )
        self.kinds = [BF] * (SUMS - 1) + [F32]
        steps = [step] * (SUMS - 1) + [step // 2]
        self.rows = [-(-rows // each) * each for rows, each in zip(self.filled, steps)]
        self.windows = [window(i, i + ROWS, self.length, self.tile) for i in range(0, self.length, ROWS)]

    def reserve(self, group, rows):
        self.filled[group] += rows
        return group, self.filled[group] - rows


class Links:
    def __init__(self, far, send, receive):
        img, blk = lax.axis_index("img"), lax.axis_index("blk")
        self.far = far
        self.z, self.y, self.x, self.c = img // 2, img % 2, blk // 2, blk % 2
        self.send, self.receive, self.used, self.started = send, receive, 0, []

    def device(self, z, y, x, c):
        return (z * 2 + y, x * 2 + c)

    def mate(self):
        return self.device(self.z, self.y, self.x, 1 - self.c)

    def along(self, turn):
        return self.device(self.z, (self.y + turn) % 2, (self.x + 1 - turn) % 2, self.c)

    def level(self, k):
        return self.device((self.z + k) % self.far, self.y, self.x, self.c)

    def block(self, k):
        x, c = (self.x + k // 2) % 2, (self.c + k % 2) % 2
        return self.device(self.z, self.y, x, c), x * 2 + c

    def copy(self, source, target, device):
        i = self.used
        self.used += 1
        made = pltpu.make_async_remote_copy(
            src_ref=source, dst_ref=target, send_sem=self.send.at[i], recv_sem=self.receive.at[i],
            device_id=device, device_id_type=MESH,
        )
        made.start()
        self.started.append(made)
        return made

    def enter(self, meanwhile):
        barrier = pltpu.get_barrier_semaphore()
        partners = [self.block(k)[0] for k in (1, 2, 3)] + [self.along(1)]
        partners += [self.level(k) for k in range(1, self.far)]
        for partner in partners:
            pl.semaphore_signal(barrier, inc=1, device_id=partner, device_id_type=MESH)
        meanwhile()
        pl.semaphore_wait(barrier, len(partners))

    def finish(self):
        for made in self.started:
            made.wait_send()


def add_rows(target, start, other, other_start, count, step):
    def one(i, _):
        a = pl.ds(pl.multiple_of(start + i * step, 8), step)
        b = pl.ds(pl.multiple_of(other_start + i * step, 8), step)
        target[a, :] = (target[a, :].astype(F32) + other[b, :].astype(F32)).astype(target.dtype)
        return 0

    lax.fori_loop(0, count // step, one, 0)


class Level:
    def __init__(self, links, turn, flat, deep):
        self.links, self.turn, self.flat = links, turn, flat
        self.deep = links.far if deep else 1
        self.size = flat * self.deep

    def place(self, x, y, z):
        if self.flat == 1:
            at = 0
        elif self.turn is None:
            at = x * 2 + y
        else:
            at = x * (1 - self.turn) + y * self.turn
        return at * self.deep + (z if self.deep > 1 else 0)

    def mine(self):
        return self.place(self.links.x, self.links.y, self.links.z)

    def partner(self, k, back=1):
        t = self.links
        flat, z = k // self.deep, (t.z + back * (k % self.deep) + t.far) % t.far
        if self.flat == 1:
            x, y = t.x, t.y
        elif self.turn is None:
            x, y = (t.x + flat // 2) % 2, (t.y + flat % 2) % 2
        else:
            x, y = (t.x + (1 - self.turn) * flat) % 2, (t.y + self.turn * flat) % 2
        return t.device(z, y, x, t.c), self.place(x, y, z)


def levels_of(links, kind, core):
    both, deep = Level(links, None, 4, False), Level(links, 0, 1, True)
    x, y = Level(links, 0, 2, False), Level(links, 1, 2, False)
    if kind == TURNS:
        return [Level(links, core, 2, False), Level(links, 1 - core, 2, False), deep]
    return {FLAT: [both, deep], Y_FIRST: [y, x, deep], ALL: [Level(links, None, 4, True)], Y_DEEP: [y, deep, x]}[kind]


TURNS, FLAT, Y_FIRST, ALL, Y_DEEP = range(5)


def sum_group(links, kind, rows, buf, out, mate_in, level_in, own, own_sem):
    c = links.c
    levels = levels_of(links, kind, c)
    first_of_mate = levels_of(links, kind, 1 - c)[0]
    mate = links.mate()
    half = rows // 2
    n = half // (4 * links.far)

    def part(ref, start, size):
        return ref.at[pl.ds(pl.multiple_of(start, 8), size), :]

    def ordered(level, core_level):
        k = level.size
        return [core_level.partner(j)[1] for j in range(1, k)] + [core_level.mine()]

    base, size = c * half, half
    cut = levels[0].size if levels[0].size <= 4 else 1
    sub = half // cut
    pending = []
    to_mate = ordered(levels[0], first_of_mate) if cut > 1 else [0]
    for at in to_mate:
        pending.append([(links.copy(part(buf, (1 - c) * half + at * sub, sub), part(mate_in, at * sub, sub), mate), mate_in)])
    where = ordered(levels[0], levels[0]) if cut > 1 else [0]
    recv_at = 0
    for i, level in enumerate(levels):
        yield
        step = size // level.size
        following = levels[i + 1] if i + 1 < len(levels) else None
        split = level.size == 2 and following is not None and following.size == 2
        sent = [[], []] if split else [[]]
        spots = [level.partner(k)[1] for k in range(1, level.size)]

        def send(k):
            device, at = level.partner(k)
            slot = recv_at + (k - 1) * step
            if split:
                half_step = step // 2
                for j, two in enumerate((1 - following.mine(), following.mine())):
                    sent[j].append((links.copy(
                        part(buf, base + at * step + two * half_step, half_step),
                        part(level_in, slot + two * half_step, half_step), device), level_in, slot + two * half_step))
            else:
                sent[0].append((links.copy(part(buf, base + at * step, step), part(level_in, slot, step), device), level_in, slot))

        def take(group, at, count, first_in):
            for made in group:
                made[0].wait_recv()
                start = made[2] if len(made) > 2 else first_in
                add_rows(buf, base + at * count, made[1], start, count, min(count, 8 * n))

        if len(pending) == level.size:
            for k, (group, at) in enumerate(zip(pending, where), 1):
                take(group, at, step, at * step)
                if k < level.size:
                    send(k)
        else:
            for group in pending:
                take(group, 0, size, 0)
            for k in range(1, level.size):
                send(k)
        recv_at += (level.size - 1) * step
        base, size = base + level.mine() * step, step
        pending = sent
        where = [1 - following.mine(), following.mine()] if split else [0]
    yield
    total = buf[pl.ds(pl.multiple_of(base, 8), n), :].astype(F32)
    for made, ref, slot in pending[0]:
        made.wait_recv()
        total += ref[pl.ds(pl.multiple_of(slot, 8), n), :].astype(F32)
    own[...] = total.astype(own.dtype)
    at = part(out, base, n)
    local = pltpu.make_async_copy(own, at, own_sem)
    local.start()
    inner = levels[-1]
    back = [links.copy(own, at, inner.partner(k)[0]) for k in range(1, inner.size)]
    yield
    for made in back:
        made.wait_recv()
    local.wait()
    piece = n * inner.size
    base = base - inner.mine() * n
    outer = levels[:-1]
    flying = [[] for _ in outer]
    to_mate = []

    def pass_on(start, level_count):
        whole = part(out, start, piece)
        for i in reversed(range(level_count)):
            for k in range(1, outer[i].size):
                flying[i].append((k, links.copy(whole, whole, outer[i].partner(k)[0]), start))
        to_mate.append(links.copy(whole, whole, mate))

    pass_on(base, len(outer))
    step = piece
    for i in reversed(range(len(outer))):
        yield
        level = outer[i]
        for k, made, start in list(flying[i]):
            made.wait_recv()
            pass_on(start + (level.partner(k, -1)[1] - level.mine()) * step, i)
        step *= level.size
    yield
    for made in to_mate:
        made.wait_recv()


def layer_kernel(z, names, *refs):
    r = SimpleNamespace(**dict(zip(names, refs)))
    length, model, axis, pairs = z.length, z.model, z.axis, z.pairs
    tile, width = z.tile, z.width
    chunks = z.hidden // model
    links = Links(z.far, r.send, r.receive)
    mine = links.x * 2 + links.c
    local_used = [0]

    def local_copy(source, target):
        i = local_used[0]
        local_used[0] += 1
        made = pltpu.make_async_copy(source, target, r.load.at[i])
        made.start()
        return made

    small_loads = [
        local_copy(source, target)
        for source, target in ((r.keep_in, r.keep_in_v), (r.noise, r.noise_v), (r.grad_keep, r.grad_keep_v))
    ]
    w = SimpleNamespace(**{n: getattr(r, n + VALUE) for n in LOADED})
    given = w
    small_send, small = r.small_send, r.small

    def collect():
        for made in small_loads:
            made.wait()
        for s in range(axis):
            small_send[s, 0:1, :] = r.keep_in_v[s].astype(F32)
            small_send[s, 1:3, :] = r.noise_v[s]
            small_send[s, 3:4, :] = r.grad_keep_v[s]
            small_send[s, 4:8, :] = jnp.zeros((4, width), F32)

    links.enter(collect)

    def spread(source, target):
        return [links.copy(source.at[links.block(k)[1]], target.at[:, mine], links.block(k)[0]) for k in (2, 3, 1)]

    small_copies = [links.copy(small_send.at[links.block(k)[1]], small.at[mine], links.block(k)[0]) for k in (2, 3, 1)]
    token_copies = spread(r.tokens, r.tok)
    loads = {n: local_copy(getattr(r, n), getattr(r, n + VALUE)) for n in LOADED}
    token_local = local_copy(r.tokens.at[mine], r.tok.at[:, mine])
    grad_local = local_copy(r.grad_out.at[mine], r.gout.at[:, mine])
    small[mine] = small_send[mine]

    ends = []
    total = 0
    for i in range(z.images):
        total = total + r.lengths[mine, i]
        ends.append(total)
    place = Place(axis, length, ends)

    meta, kept_row, vec = r.meta, r.kept_row, r.vec
    vec[...] = jnp.zeros_like(vec)
    groups = [r.buf0, r.buf1, r.buf2, r.buf3, r.buf4, r.buf5, r.buf6]
    for g in range(SUMS):
        if z.filled[g] < z.rows[g]:
            groups[g][z.filled[g] :, :] = jnp.zeros((z.rows[g] - z.filled[g], 128), z.kinds[g])
    for made in small_copies:
        made.wait_recv()
    for p in range(axis):
        block = jnp.concatenate([small[p], jnp.zeros((120, width), F32)], 0).T
        for t in range(z.tiles):
            meta[t * tile + p * CHUNK : t * tile + (p + 1) * CHUNK, :] = block[t * CHUNK : (t + 1) * CHUNK, :]
    for t in range(length // 128):
        kept_row[:, t * 128 : (t + 1) * 128] = meta[t * 128 : (t + 1) * 128, :].T[0:8]

    bias = [r.bias0, r.bias1, r.bias2, r.bias3]
    bias_back = [r.back0, r.back1, r.back2, r.back3]
    for i, (low, high) in enumerate(z.windows):
        span = high - low
        for back in (False, True):
            spot_q = place.row(i * ROWS, ROWS) if back else place.column(i * ROWS, ROWS)
            spot_k = place.column(low, span) if back else place.row(low, span)
            kept_k = meta[low:high, 0:1] if back else kept_row[0:1, low:high]
            segment_k = jnp.where((kept_k > 0) & (spot_k < ends[-1]), place.segments(spot_k), -1)
            allowed = (place.segments(spot_q) == segment_k) | (spot_q == spot_k)
            (bias_back if back else bias)[i][...] = jnp.where(allowed, 0.0, NEG)

    def vec_set(at, value):
        vec[at : at + 1, : value.shape[1]] = value

    def put(where, value, rows=0):
        group, at = where
        value = value.astype(z.kinds[group])
        for j in range(value.shape[1] // 128):
            groups[group][at + rows : at + rows + value.shape[0], :] = value[:, j * 128 : (j + 1) * 128]
            rows += value.shape[0]

    def row(ref):
        return ref[...].reshape(1, -1)

    def flat(ref):
        return ref[...].reshape(length, model)

    def tiled(ref, value):
        ref[...] = value.reshape(z.tiles, axis, CHUNK, model)

    spot = place.column(0, length)
    segment = place.segments(spot)
    live = (spot < ends[-1]).astype(F32)
    kept = jnp.where(meta[:, 0:1] > 0, live, 0.0)
    member = (segment == lanes(128)).astype(F32)
    r.member[...] = member.astype(BF)
    r.chosen[...] = (member * kept).astype(BF)

    for n in (LARGE[0], WEIGHTS[0], WEIGHTS[1]):
        loads.pop(n).wait()
    token_local.wait()
    for made in token_copies:
        made.wait_recv()
    grad_copies = spread(r.grad_out, r.gout)

    unit, _s = normalise(flat(r.tok).astype(F32))
    low = (unit * row(given.first_gain) + row(given.first_shift)).astype(BF)
    r.normed[...] = low
    r.query[...] = (dot(low, w.qkv_weight[:, :model]) * 0.125).astype(BF)
    key = dot(low, w.qkv_weight[:, model : 2 * model]).astype(BF)
    value = dot(low, w.qkv_weight[:, 2 * model :]).astype(BF)
    ones = jnp.ones((length, 128), BF)
    for p in range(pairs):
        for ref, kind in ((r.key_ones, key), (r.value_ones, value)):
            ref[:, p * 256 : p * 256 + 128] = kind[:, p * 128 : (p + 1) * 128]
            ref[:, p * 256 + 128 : (p + 1) * 256] = ones

    half = lanes(128) < HEAD
    for i, (low, high) in enumerate(z.windows):
        rows = slice(i * ROWS, (i + 1) * ROWS)
        for p in range(pairs):
            at = slice(p * 128, (p + 1) * 128)
            q = r.query[rows, at]
            outs, logs = [], []
            for side in (half, ~half):
                masked = jnp.where(side, q, jnp.zeros_like(q))
                scores = dot_nt(masked, r.key_ones[low:high, p * 256 : p * 256 + 128]) + bias[i][...]
                top = jnp.max(scores, -1, keepdims=True)
                weights = jnp.exp(scores - top).astype(BF)
                both = dot(weights, r.value_ones[low:high, p * 256 : (p + 1) * 256])
                outs.append(both[:, :128] / both[:, 128:])
                logs.append(top + jnp.log(both[:, 128:]))
            r.heads_out[rows, at] = jnp.where(half, outs[0], outs[1])
            r.lse_parts[rows, at] = features(-jnp.where(half, logs[0], logs[1]))

    for made in loads.values():
        made.wait()

    low = r.heads_out[...].astype(BF)
    r.attended[...] = low
    hid = flat(r.tok).astype(F32) + dot(low, w.proj_weight[...]) + row(given.proj_bias)
    r.hidden[...] = hid
    unit, _s = normalise(hid)
    low = (unit * row(given.second_gain) + row(given.second_shift)).astype(BF)
    r.normed_two[...] = low
    expand_bias = row(given.expand_bias)
    for c in range(chunks):
        at = slice(c * model, (c + 1) * model)
        act, slope = gelu_pair(dot(low, w.expand_weight[:, at]) + expand_bias[:, at])
        r.active[:, at] = act.astype(BF)
        r.expand_low[:, at] = slope.astype(BF)
    blk = hid + dot(r.active[...], w.reduce_weight[...]) + row(given.reduce_bias)
    r.block[...] = blk
    tiled(r.out_v, (blk * live).astype(BF))
    unit, _s = normalise(blk)
    low = (unit * row(given.score_gain) + row(given.score_shift)).astype(BF)
    r.score_in[...] = low
    act, slope = gelu_pair(dot(low, w.score_weight[...]) + row(given.score_bias))
    r.score_act[...] = act
    r.score_slope[...] = slope

    returned, locals_left = [], []

    def give_back(source, target):
        locals_left.append(local_copy(source.at[:, mine], target.at[mine]))
        for k in (2, 3, 1):
            device, at = links.block(k)
            returned.append(links.copy(source.at[:, at], target.at[mine], device))

    give_back(r.out_v, r.out_tokens)

    one, two = split_two(act)
    sums = dot_tn(r.chosen[...], one) + dot_tn(r.chosen[...], two)
    counts = dot_tn(r.chosen[...], jnp.ones((length, 128), BF))
    inverse = jnp.tile(1.0 / jnp.maximum(counts, 1.0), (1, pairs))
    one, two = split_two(sums * inverse)
    local_columns = lanes(model) < model // 2
    weight_gap = w.last_weight[0:1, :].astype(F32) - w.last_weight[1:2, :].astype(F32)
    bias_gap = r.last_bias[0] - r.last_bias[1]

    spread_mean = dot(r.member[...], one) + dot(r.member[...], two)
    join = jnp.where(local_columns, r.score_act[...], spread_mean).astype(BF)
    r.joined[...] = join
    act, pred_slope = gelu_pair(dot_nt(join, w.pred_weight[...]) + row(given.pred_bias))
    pred_low = act.astype(BF)
    r.pred_act[...] = pred_low
    act, mid_slope = gelu_pair(dot(pred_low, w.mid_weight[...]) + row(given.mid_bias))
    mid_low = act.astype(BF).astype(F32)
    info = meta[...]
    margin = jnp.sum(mid_low * weight_gap, -1, keepdims=True) + bias_gap + info[:, 1:2] - info[:, 2:3]
    sig = 1.0 / (1.0 + jnp.exp(-margin))
    r.keep_col[...] = jnp.broadcast_to(sig * kept, (length, 128))
    margin_grad = info[:, 3:4] * kept * sig * (1.0 - sig)
    vec_set(VEC.last_weight, jnp.sum(mid_low * margin_grad, 0, keepdims=True))
    vec_set(VEC.last_bias, jnp.sum(jnp.broadcast_to(margin_grad, (length, 128)), 0, keepdims=True))
    mid_grad = (margin_grad * weight_gap * mid_slope).astype(BF)
    r.mid_grad_low[...] = mid_grad
    vec_set(VEC.mid_bias, total_rows(mid_grad))
    pred_grad = (dot_nt(mid_grad, w.mid_weight[...]) * pred_slope).astype(BF)
    r.pred_grad_low[...] = pred_grad
    vec_set(VEC.pred_bias, total_rows(pred_grad))
    join_grad = dot(pred_grad, w.pred_weight[...])
    r.score_act[...] = join_grad
    one, two = split_two(join_grad)
    mean_grad = dot_tn(r.member[...], one) + dot_tn(r.member[...], two)
    grad_one, grad_two = split_two(mean_grad * inverse)

    for p in range(axis):
        parts = [r.keep_col[t * tile + p * CHUNK : t * tile + (p + 1) * CHUNK, :] for t in range(z.tiles)]
        r.keep_v[p] = jnp.concatenate(parts, 0).T[0:8]
    for k in (2, 3, 1):
        device, at = links.block(k)
        returned.append(links.copy(r.keep_v.at[at], r.keep.at[mine], device))
    locals_left.append(local_copy(r.keep_v.at[mine], r.keep.at[mine]))

    def summing(g, names):
        return sum_group(links, KINDS[g], z.rows[g], *[getattr(r, n + str(g)) for n in names], r.own_sem.at[g])

    sum_names = names_of(buf=0, sum=0, mate_in=0, level_in=0, own=0)
    running = [summing(g, sum_names) for g in range(SUMS)]

    def advance(*which):
        for g in which:
            next(running[g], None)

    def point(i):
        advance(*PLAN.get(i, ()))

    spread_grad = dot(r.chosen[...], grad_one) + dot(r.chosen[...], grad_two)
    low = (jnp.where(local_columns, r.score_act[...], spread_grad) * r.score_slope[...]).astype(BF)
    r.score_grad_low[...] = low
    vec_set(VEC.score_bias, total_rows(low))
    put(z.at.score, dot_tn(r.score_in[...], low))
    put(z.at.pred, dot_tn(r.pred_grad_low[...], r.joined[...]))
    mid = dot_tn(r.pred_act[...], r.mid_grad_low[...])
    put(z.at.mid, jnp.concatenate([mid, jnp.zeros((model // 2, 128 - z.mid), F32)], 1))
    advance(0)

    grad_local.wait()
    for made in grad_copies:
        made.wait_recv()
    grad = dot_nt(r.score_grad_low[...], w.score_weight[...])
    unit, scale = normalise(r.block[...])
    vec_set(VEC.score_gain, jnp.sum(grad * unit, 0, keepdims=True))
    vec_set(VEC.score_shift, jnp.sum(grad, 0, keepdims=True))
    blk_grad = norm_back(grad, unit, scale, row(given.score_gain)) + flat(r.gout).astype(F32) * live
    r.block[...] = blk_grad
    low = blk_grad.astype(BF)
    r.block_low[...] = low
    vec_set(VEC.reduce_bias, total_rows(low))
    point(0)
    for c in range(chunks):
        part = dot_tn(r.active[:, c * model : (c + 1) * model], r.block_low[...]).astype(BF)
        for j in range(pairs):
            put(z.at.reduce, part[:, j * 128 : (j + 1) * 128], j * z.hidden + c * model)
        point(30 + c)
    advance(1)
    point(1)
    for c in range(chunks):
        at = slice(c * model, (c + 1) * model)
        piece = (dot_nt(r.block_low[...], w.reduce_weight[at, :]) * r.expand_low[:, at].astype(F32)).astype(BF)
        r.expand_low[:, at] = piece
        vec_set(VEC.expand_bias + c, total_rows(piece))
        put(z.at.expand, dot_tn(r.normed_two[...], piece), c * pairs * model)
        if c + 1 == chunks:
            advance(2)
        point(2 + c)

    grad = dot_nt(r.expand_low[...], w.expand_weight[...])
    unit, scale = normalise(r.hidden[...])
    vec_set(VEC.second_gain, jnp.sum(grad * unit, 0, keepdims=True))
    vec_set(VEC.second_shift, jnp.sum(grad, 0, keepdims=True))
    hid_grad = norm_back(grad, unit, scale, row(given.second_gain)) + r.block[...]
    r.hidden[...] = hid_grad
    low = hid_grad.astype(BF)
    r.hidden_low[...] = low
    vec_set(VEC.proj_bias, total_rows(low))
    point(40)
    low = dot_nt(low, w.proj_weight[...]).astype(BF)
    r.attended_grad[...] = low
    one, two = split_two(low.astype(F32) * r.heads_out[...])
    pair_sum = (
        lax.broadcasted_iota(jnp.int32, (128, 128), 0) // HEAD == lax.broadcasted_iota(jnp.int32, (128, 128), 1) // HEAD
    ).astype(BF)
    for p in range(pairs):
        at = slice(p * 128, (p + 1) * 128)
        r.delta_parts[:, at] = features(-(dot(one[:, at], pair_sum) + dot(two[:, at], pair_sum)))
    point(6)
    put(z.at.proj, dot_tn(r.attended[...], r.hidden_low[...]))
    point(7)

    key_grad, value_grad = r.block, r.score_act
    key_grad[...] = jnp.zeros_like(key_grad)
    value_grad[...] = jnp.zeros_like(value_grad)
    unit_count = 0
    for p in range(pairs):
        at = slice(p * 128, (p + 1) * 128)
        wide = slice(p * 256, (p + 1) * 256)
        near = slice(p * 256, p * 256 + 128)
        for i, (low, high) in enumerate(z.windows):
            rows = slice(i * ROWS, (i + 1) * ROWS)
            q, lse, og, delta = r.query[rows, at], r.lse_parts[rows, at], r.attended_grad[rows, at], r.delta_parts[rows, at]
            zero = jnp.zeros_like(q)
            query_parts, key_part, value_part = [], 0, 0
            for side in (half, ~half):
                mq, mo = jnp.where(side, q, zero), jnp.where(side, og, zero)
                wide_q = jnp.concatenate([mq, jnp.where(side, lse, zero)], 1)
                wide_o = jnp.concatenate([mo, jnp.where(side, delta, zero)], 1)
                probs = jnp.exp(dot_nt(r.key_ones[low:high, wide], wide_q) + bias_back[i][...])
                score_grad = (probs * dot_nt(r.value_ones[low:high, wide], wide_o)).astype(BF)
                value_part += dot(probs.astype(BF), mo)
                key_part += dot(score_grad, mq)
                query_parts.append(dot_tn(score_grad, r.key_ones[low:high, near]))
            value_grad[low:high, at] += value_part
            key_grad[low:high, at] += key_part
            r.query_grad[rows, at] = (jnp.where(half, query_parts[0], query_parts[1]) * 0.125).astype(BF)
            point(8 + unit_count)
            unit_count += 1
        three = jnp.concatenate([r.query_grad[:, at], key_grad[:, at].astype(BF), value_grad[:, at].astype(BF)], 1)
        put(z.at.qkv[p], dot_tn(r.normed[...], three))
        if p + 1 == pairs or z.at.qkv[p + 1][0] != z.at.qkv[p][0]:
            advance(z.at.qkv[p][0])
    point(20)

    parts = jnp.concatenate([r.query_grad[...], key_grad[...].astype(BF), value_grad[...].astype(BF)], 1)
    grad = dot_nt(parts, w.qkv_weight[...])
    point(41)
    unit, scale = normalise(flat(r.tok).astype(F32))
    vec_set(VEC.first_gain, jnp.sum(grad * unit, 0, keepdims=True))
    vec_set(VEC.first_shift, jnp.sum(grad, 0, keepdims=True))
    put(z.at.vec, vec[...])
    advance(6)
    tiled(r.grad_v, (norm_back(grad, unit, scale, row(given.first_gain)) + r.hidden[...]).astype(BF))
    give_back(r.grad_v, r.tokens_grad)
    point(21)
    advance(*PLAN_END)
    for _ in range(20):
        advance(*range(SUMS))
    for made in returned:
        made.wait_recv()
    for made in locals_left:
        made.wait()
    links.finish()


VALUE = "_v"
KINDS = (Y_FIRST, TURNS, TURNS, TURNS, TURNS, FLAT, ALL)
PLAN = {31: (0,), 4: (1,), 40: (0,), 6: (2,), 9: (1,), 10: (0,), 13: (1, 2, 3), 15: (0,), 17: (4,), 18: (2, 3), 19: (1,), 20: (0,), 41: (4, 5), 21: (3,)}
PLAN_END = (0, 6, 4, 2, 1, 5, 0, 3, 0, 4, 1, 6, 5, 2, 3, 4, 5, 6, 1, 6, 2, 4, 3, 1, 5, 5, 4, 4, 3, 2, 3, 2)


def run_layer(z, tokens, grad_out, keep_in, noise, grad_keep, lengths, weights):
    L, D, U = z.length, z.model, z.hidden
    half = D // 2
    sm, far = (pl.BlockSpec(memory_space=m) for m in (pltpu.SMEM, pl.ANY))
    inputs = dict(
        tokens=(tokens, far), grad_out=(grad_out, far), keep_in=(keep_in, far), noise=(noise, far),
        grad_keep=(grad_keep, far), lengths=(lengths, sm),
    )
    for n in WEIGHTS:
        inputs[n] = (weights[n], sm if n == LAST_BIAS else far)
    four = jax.ShapeDtypeStruct((z.axis, z.tiles, CHUNK, D), BF)
    outs = dict(out_tokens=four, keep=jax.ShapeDtypeStruct((z.axis, 8, z.width), F32), tokens_grad=four)
    low = lambda *s: VMEM(s, BF)
    full = lambda *s: VMEM(s, F32)
    tiles = low(z.tiles, z.axis, CHUNK, D)
    small = full(z.axis, 8, z.width)
    scratch = dict(
        tok=tiles, gout=tiles, out_v=tiles, grad_v=tiles, small_send=small, small=small, keep_v=small,
        meta=full(L, 128), kept_row=full(8, L), member=low(L, 128), chosen=low(L, 128),
        normed=low(L, D), query=low(L, D), key_ones=low(L, 2 * D), value_ones=low(L, 2 * D),
        heads_out=full(L, D), lse_parts=low(L, D), delta_parts=low(L, D), attended=low(L, D),
        hidden=full(L, D), normed_two=low(L, D), active=low(L, U), expand_low=low(L, U),
        block=full(L, D), score_in=low(L, D), score_act=full(L, D), score_slope=full(L, D),
        joined=low(L, D), pred_act=low(L, half), mid_grad_low=low(L, z.mid), pred_grad_low=low(L, half),
        score_grad_low=low(L, D), block_low=low(L, D), hidden_low=low(L, D), attended_grad=low(L, D),
        query_grad=low(L, D), vec=full(VEC_ROWS, D), keep_col=full(L, 128),
    )
    for n in LOADED:
        scratch[n + VALUE] = VMEM(weights[n].shape, weights[n].dtype)
    scratch.update(keep_in_v=VMEM(keep_in.shape, jnp.int32), noise_v=full(*noise.shape), grad_keep_v=full(*grad_keep.shape))
    for i, (first, last) in enumerate(z.windows):
        scratch.update(zip(("bias%d" % i, "back%d" % i), (full(ROWS, last - first), full(last - first, ROWS))))
    sum_names = names_of(sum=0, buf=0, mate_in=0, level_in=0, own=0)
    for g, (rows, kind) in enumerate(zip(z.rows, z.kinds)):
        n = rows // (8 * z.far)
        shapes = [(rows, 128), (rows, 128), (rows // 2, 128), (rows // 2 - n, 128), (n, 128)]
        outs[sum_names[0] + str(g)] = jax.ShapeDtypeStruct(shapes[0], kind)
        scratch.update((name + str(g), VMEM(shape, kind)) for name, shape in zip(sum_names[1:], shapes[1:]))
    sems = 12 + SUMS * 36
    scratch.update(send=DMA((sems,)), receive=DMA((sems,)), load=DMA((len(LOADED) + 8,)), own_sem=DMA((SUMS,)))
    results = pl.pallas_call(
        functools.partial(layer_kernel, z, tuple(inputs) + tuple(outs) + tuple(scratch)),
        out_shape=list(outs.values()),
        in_specs=[spec for _, spec in inputs.values()],
        out_specs=[far] * len(outs),
        scratch_shapes=list(scratch.values()),
        compiler_params=pltpu.CompilerParams(collective_id=0, has_side_effects=True, vmem_limit_bytes=63 * 2**20),
        name="layer",
    )(*[array for array, _ in inputs.values()])
    return dict(zip(outs, results))


STAGED = names_of(reduce_weight=0, score_weight=0, pred_weight=0, expand_weight=0, proj_weight=0, qkv_weight=0)
PASSED = names_of(out_tokens=0, tokens_grad=0)


def unpack_kernel(z, names, *refs):
    r = SimpleNamespace(**dict(zip(names, refs)))
    out = SimpleNamespace(**{n: getattr(r, n + VALUE) if n in STAGED else getattr(r, n) for n in WEIGHTS})
    sums = [r.in0, r.in1, r.in2, r.in3, r.in4, r.in5, r.in6]
    used = [0]

    def start(source, target):
        made = pltpu.make_async_copy(source, target, r.sem.at[used[0]])
        used[0] += 1
        made.start()
        return made

    loads = [start(source, ref) for source, ref in zip((r.sum0, r.sum1, r.sum2, r.sum3, r.sum4, r.sum5, r.sum6), sums)]
    through = [start(r.out_tokens, r.out_tokens_v), start(r.tokens_grad, r.tokens_grad_v)]
    stored = []
    model, pairs, half = z.model, z.pairs, z.model // 2

    def take(where, first, count):
        group, at = where
        return sums[group][at + first : at + first + count, :].astype(F32)

    def store(*names):
        stored.extend(start(getattr(r, n + VALUE), getattr(r, n)) for n in names)

    loads[0].wait()
    for j in range(pairs):
        at = slice(j * 128, (j + 1) * 128)
        out.score_weight[:, at] = take(z.at.score, j * model, model)
        out.pred_weight[:, at] = take(z.at.pred, j * half, half)
    out.mid_weight[...] = take(z.at.mid, 0, half)[:, : z.mid]
    store(STAGED[1], STAGED[2])
    loads[1].wait()
    for j in range(pairs):
        out.reduce_weight[:, j * 128 : (j + 1) * 128] = take(z.at.reduce, j * z.hidden, z.hidden)
    store(STAGED[0])
    loads[2].wait()
    for j in range(z.hidden // 128):
        out.expand_weight[:, j * 128 : (j + 1) * 128] = take(z.at.expand, j * model, model)
    store(STAGED[3])
    through[0].wait()
    through[1].wait()
    stored.append(start(r.out_tokens_v, r.out_tokens_out))
    stored.append(start(r.tokens_grad_v, r.tokens_grad_out))
    loads[3].wait()
    loads[4].wait()
    loads[5].wait()
    for j in range(pairs):
        out.proj_weight[:, j * 128 : (j + 1) * 128] = take(z.at.proj, j * model, model)
        for t in range(3):
            at = t * model + j * 128
            out.qkv_weight[:, at : at + 128] = take(z.at.qkv[j], t * model, model)
    store(STAGED[4], STAGED[5])
    loads[6].wait()
    vec = jnp.concatenate([take(z.at.vec, j * VEC_ROWS, VEC_ROWS) for j in range(pairs)], 1)

    def row(at):
        return vec[at : at + 1, :]

    chunks = z.hidden // model
    for ref, at in (
        (out.first_gain, VEC.first_gain), (out.first_shift, VEC.first_shift), (out.proj_bias, VEC.proj_bias),
        (out.second_gain, VEC.second_gain), (out.second_shift, VEC.second_shift), (out.reduce_bias, VEC.reduce_bias),
        (out.score_gain, VEC.score_gain), (out.score_shift, VEC.score_shift), (out.score_bias, VEC.score_bias),
    ):
        ref[...] = row(at).reshape(model)
    out.expand_bias[...] = jnp.concatenate([row(VEC.expand_bias + c) for c in range(chunks)], 1).reshape(z.hidden)
    out.pred_bias[...] = row(VEC.pred_bias)[:, :half].reshape(half)
    out.mid_bias[...] = row(VEC.mid_bias)[:, : z.mid].reshape(z.mid)
    gap = row(VEC.last_weight)[:, : z.mid]
    out.last_weight[...] = jnp.concatenate([gap, -gap], 0)
    gap = row(VEC.last_bias)[:, 0:2]
    out.last_bias[...] = jnp.where(lanes(2) == 0, gap, -gap).reshape(2)
    for s in range(z.axis):
        r.keep_out[s] = r.keep[s, 0:1, :]
    for made in stored:
        made.wait()


def run_unpack(z, results, shapes):
    far, vm = pl.BlockSpec(memory_space=pl.ANY), pl.BlockSpec(memory_space=pltpu.VMEM)
    tokens = results[PASSED[0]]
    outs = dict(
        out_tokens_out=(tokens, far), keep_out=(jax.ShapeDtypeStruct((z.axis, 1, z.width), F32), vm),
        tokens_grad_out=(tokens, far),
    )
    for n in WEIGHTS:
        outs[n] = (jax.ShapeDtypeStruct(shapes[n], F32), far if n in STAGED else vm)
    scratch = dict(out_tokens_v=VMEM(tokens.shape, BF), tokens_grad_v=VMEM(tokens.shape, BF))
    for g in range(SUMS):
        scratch["in%d" % g] = VMEM((z.rows[g], 128), z.kinds[g])
    for n in STAGED:
        scratch[n + VALUE] = VMEM(shapes[n], F32)
    scratch.update(sem=DMA((SUMS + 4 + len(STAGED),)))
    done = pl.pallas_call(
        functools.partial(unpack_kernel, z, tuple(results) + tuple(outs) + tuple(scratch)),
        out_shape=[jax.ShapeDtypeStruct(s.shape, s.dtype) for s, _ in outs.values()],
        in_specs=[far, vm] + [far] * (SUMS + 1),
        out_specs=[spec for _, spec in outs.values()],
        scratch_shapes=list(scratch.values()),
        compiler_params=pltpu.CompilerParams(vmem_limit_bytes=63 * 2**20),
        name="unpack",
    )(*results.values())
    return done


def per_device(tokens, lengths, keep_in, noise, *rest):
    weights, (grad_out, grad_keep) = dict(zip(WEIGHTS, rest[:21])), rest[21:]
    slots, width, _, model = tokens.shape
    w = SimpleNamespace(**weights)
    z = Sizes(
        slots, lax.axis_size("img"), width, model, w.expand_weight.shape[1], w.mid_weight.shape[1], lengths.shape[1]
    )
    turned = names_of(pred_weight=0, last_weight=0)
    for n in turned:
        weights[n] = weights[n].T
    four = (slots, width // CHUNK, CHUNK, model)
    results = run_layer(
        z, tokens.reshape(four), grad_out.reshape(four), keep_in.reshape(slots, 1, width),
        noise.reshape(slots, width, 2).swapaxes(1, 2), grad_keep.reshape(slots, 1, width), lengths, weights,
    )
    done = run_unpack(z, results, {n: v.shape for n, v in weights.items()})
    back = dict(zip(WEIGHTS, done[3:]))
    for n in turned:
        back[n] = back[n].T
    return (
        done[0].reshape(tokens.shape), done[1].reshape(keep_in.shape), done[2].reshape(tokens.shape)
    ) + tuple(back.values())


def solution(mesh):
    split = P("img", None, "blk", None)
    placed = (split, P("img", None), P("img", None, "blk"), split) + (P(),) * 21 + (split, P("img", None, "blk"))

    def chosen_device(*arrays):
        return (per_device if arrays[0].shape[0] == mesh.shape["blk"] == 4 else general_device)(*arrays)

    return jax.shard_map(
        chosen_device, mesh=mesh, in_specs=placed, out_specs=(split, P("img", None, "blk"), split) + (P(),) * 21,
        check_vma=False,
    )
```

```python
import functools
import math
from types import SimpleNamespace

import jax
import jax.numpy as jnp
from jax import lax
from jax.experimental import pallas as pl
from jax.experimental.pallas import tpu as pltpu
from jax.sharding import PartitionSpec as P

HEAD = 64

EPS = 1e-06
NEG = -1e30
HIGH = lax.Precision.HIGHEST


def layer_norm(row_data, norm_gain, norm_shift):
    centre = row_data - jnp.mean(row_data, -1, keepdims=True)
    spread = jnp.mean(centre * centre, -1, keepdims=True)
    return centre * lax.rsqrt(spread + EPS) * norm_gain + norm_shift


def gelu_exact(values):
    return jax.nn.gelu(values, approximate=False)


def matmul(former, latter):
    return jnp.dot(former, latter, preferred_element_type=jnp.float32)


def left_outer(former, latter):
    return lax.dot_general(
        former, latter, (((0,), (0,)), ((), ())), preferred_element_type=jnp.float32
    )


def right_outer(former, latter):
    return lax.dot_general(
        former, latter, (((1,), (1,)), ((), ())), preferred_element_type=jnp.float32
    )


def column_sum(values):
    return jnp.sum(values.astype(jnp.float32), 0)


def general_device(
    tokens,
    lengths,
    keep_in,
    noise,
    first_gain,
    first_shift,
    qkv_weight,
    proj_weight,
    proj_bias,
    second_gain,
    second_shift,
    expand_weight,
    expand_bias,
    reduce_weight,
    reduce_bias,
    score_gain,
    score_shift,
    score_weight,
    score_bias,
    pred_weight,
    pred_bias,
    mid_weight,
    mid_bias,
    last_weight,
    last_bias,
    grad_out,
    grad_keep,
):
    slot_count, per_slot, _, model_width = tokens.shape
    row_count = slot_count * per_slot
    head_count = model_width // HEAD
    axis_count = lax.axis_size("blk")
    axis_place = lax.axis_index("blk")
    image_ends = jnp.cumsum(lengths, 1)
    totals = image_ends[:, -1:]
    image_count = lengths.shape[1]

    def locate(places):
        segment = jnp.sum((image_ends[:, None, :] <= places[None, :, None]).astype(jnp.int32), -1)
        return (segment, places[None, :] < totals)

    query_place = jnp.arange(per_slot, dtype=jnp.int32) * axis_count + axis_place
    query_segment, query_live = locate(query_place)
    kept_mask = (keep_in[:, :, 0] > 0) & query_live
    kept_float = kept_mask.astype(jnp.float32)
    live_float = query_live.astype(jnp.float32).reshape(row_count, 1)
    kept_rows = kept_float.reshape(row_count)
    row_data = tokens.reshape(row_count, model_width).astype(jnp.float32)
    normed, first_back = jax.vjp(layer_norm, row_data, first_gain, first_shift)
    normed_low = normed.astype(jnp.bfloat16)
    qkv_rows = matmul(normed_low, qkv_weight)
    query_low = (
        (qkv_rows[:, :model_width] * 0.125)
        .astype(jnp.bfloat16)
        .reshape(slot_count, per_slot, head_count, HEAD)
    )
    key_value = (
        qkv_rows[:, model_width:]
        .astype(jnp.bfloat16)
        .reshape(slot_count, per_slot, 1, 2 * model_width)
    )
    keep_send = keep_in.astype(jnp.bfloat16)

    def scores_for(pieces):
        key_piece, keep_piece = pieces
        piece_width = key_piece.shape[2]
        key_place = (
            jnp.arange(per_slot, dtype=jnp.int32)[:, None] * axis_count
            + jnp.arange(piece_width, dtype=jnp.int32)[None, :]
        ).reshape(per_slot * piece_width)
        key_segment, key_live = locate(key_place)
        key_kept = (keep_piece.reshape(slot_count, per_slot * piece_width) > 0) & key_live
        allowed = (query_segment[:, :, None] == key_segment[:, None, :]) & key_kept[:, None, :] | (
            query_place[:, None] == key_place[None, :]
        )[None]
        split_keys = key_piece.reshape(slot_count, per_slot * piece_width, 2, head_count, HEAD)
        key_rows = split_keys[:, :, 0]
        value_rows = split_keys[:, :, 1]
        scores = jnp.einsum(
            "sqhd,skhd->shqk", query_low, key_rows, preferred_element_type=jnp.float32
        )
        return (scores, allowed[:, None], key_rows, value_rows)

    run_max = jnp.full((slot_count, head_count, per_slot), NEG, jnp.float32)
    summed = jnp.zeros((slot_count, per_slot, head_count, HEAD), jnp.float32)
    scores, allowed, key_rows, value_rows = scores_for(
        (
            lax.all_gather(key_value, "blk", axis=2, tiled=True),
            lax.all_gather(keep_send, "blk", axis=2, tiled=True),
        )
    )
    scores = jnp.where(allowed, scores, NEG)
    new_max = jnp.maximum(run_max, jnp.max(scores, -1))
    weights = jnp.where(allowed, jnp.exp(scores - new_max[..., None]), 0.0)
    factor = jnp.exp(run_max - new_max)
    update = jnp.einsum(
        "shqk,skhd->sqhd",
        weights.astype(jnp.bfloat16),
        value_rows,
        preferred_element_type=jnp.float32,
    )
    summed = summed * jnp.swapaxes(factor, 1, 2)[..., None] + update
    run_max, run_sum, summed = (new_max, jnp.sum(weights, -1), summed)
    out_heads = summed / jnp.swapaxes(run_sum, 1, 2)[..., None]
    log_total = run_max + jnp.log(run_sum)
    attended_low = out_heads.reshape(row_count, model_width).astype(jnp.bfloat16)
    hidden = row_data + matmul(attended_low, proj_weight) + proj_bias
    normed_two, second_back = jax.vjp(layer_norm, hidden, second_gain, second_shift)
    normed_two_low = normed_two.astype(jnp.bfloat16)
    expand = matmul(normed_two_low, expand_weight) + expand_bias
    active, expand_back = jax.vjp(gelu_exact, expand)
    active_low = active.astype(jnp.bfloat16)
    block = hidden + matmul(active_low, reduce_weight) + reduce_bias
    out_tokens = (block * live_float).astype(jnp.bfloat16).reshape(tokens.shape)
    score_in, score_back = jax.vjp(layer_norm, block, score_gain, score_shift)
    score_low = score_in.astype(jnp.bfloat16)
    score_pre = matmul(score_low, score_weight) + score_bias
    score_act, score_gelu_back = jax.vjp(gelu_exact, score_pre)
    half_width = score_act.shape[1] // 2
    member = (
        query_segment[:, :, None] == jnp.arange(image_count, dtype=jnp.int32)[None, None, :]
    ).astype(jnp.float32)
    chosen = member * kept_float[..., None]
    global_part = score_act[:, half_width:].reshape(slot_count, per_slot, half_width)
    part_sums = jnp.einsum("sti,stc->sic", chosen, global_part, precision=HIGH)
    part_counts = jnp.sum(chosen, 1)
    image_sums, image_counts = (
        lax.psum(part_sums.astype(jnp.bfloat16), "blk").astype(jnp.float32),
        lax.psum(part_counts.astype(jnp.bfloat16), "blk").astype(jnp.float32),
    )
    inverse = 1.0 / jnp.maximum(image_counts, 1.0)
    image_means = image_sums * inverse[..., None]
    spread_mean = jnp.einsum("sti,sic->stc", member, image_means, precision=HIGH).reshape(
        row_count, half_width
    )
    joined_low = jnp.concatenate([score_act[:, :half_width], spread_mean], 1).astype(jnp.bfloat16)
    pred_pre = matmul(joined_low, pred_weight) + pred_bias
    pred_act, pred_gelu_back = jax.vjp(gelu_exact, pred_pre)
    pred_low = pred_act.astype(jnp.bfloat16)
    mid_pre = matmul(pred_low, mid_weight) + mid_bias
    mid_act, mid_gelu_back = jax.vjp(gelu_exact, mid_pre)
    mid_low = mid_act.astype(jnp.bfloat16)
    logits = matmul(mid_low, last_weight) + last_bias
    noise_rows = noise.reshape(row_count, 2)
    margin = logits[:, 0] - logits[:, 1] + noise_rows[:, 0] - noise_rows[:, 1]
    keep_sigmoid = jax.nn.sigmoid(margin)
    keep_prob = (keep_sigmoid * kept_rows).reshape(keep_in.shape)
    margin_grad = grad_keep.reshape(row_count) * kept_rows * keep_sigmoid * (1.0 - keep_sigmoid)
    logit_grad = jnp.stack([margin_grad, -margin_grad], 1)
    last_weight_grad = lax.dot_general(
        mid_low.astype(jnp.float32), logit_grad, (((0,), (0,)), ((), ())), precision=HIGH
    )
    last_bias_grad = jnp.sum(logit_grad, 0)
    mid_grad = lax.dot_general(
        logit_grad, last_weight.astype(jnp.float32), (((1,), (1,)), ((), ())), precision=HIGH
    )
    mid_pre_low = mid_gelu_back(mid_grad)[0].astype(jnp.bfloat16)
    mid_weight_grad = left_outer(pred_low, mid_pre_low)
    mid_bias_grad = column_sum(mid_pre_low)
    pred_pre_low = pred_gelu_back(right_outer(mid_pre_low, mid_weight))[0].astype(jnp.bfloat16)
    pred_weight_grad = left_outer(joined_low, pred_pre_low)
    pred_bias_grad = column_sum(pred_pre_low)
    joined_grad = right_outer(pred_pre_low, pred_weight)
    spread_grad = joined_grad[:, half_width:].reshape(slot_count, per_slot, half_width)
    part_mean_grad = jnp.einsum("sti,stc->sic", member, spread_grad, precision=HIGH)
    mean_grad = lax.psum(part_mean_grad.astype(jnp.bfloat16), "blk").astype(jnp.float32)
    global_grad = jnp.einsum(
        "sti,sic->stc", chosen, mean_grad * inverse[..., None], precision=HIGH
    ).reshape(row_count, half_width)
    act_grad = jnp.concatenate([joined_grad[:, :half_width], global_grad], 1)
    score_pre_low = score_gelu_back(act_grad)[0].astype(jnp.bfloat16)
    score_weight_grad = left_outer(score_low, score_pre_low)
    score_bias_grad = column_sum(score_pre_low)
    block_pred_grad, score_gain_grad, score_shift_grad = score_back(
        right_outer(score_pre_low, score_weight)
    )
    block_grad = (
        block_pred_grad + grad_out.reshape(row_count, model_width).astype(jnp.float32) * live_float
    )
    block_low = block_grad.astype(jnp.bfloat16)
    reduce_weight_grad = left_outer(active_low, block_low)
    reduce_bias_grad = column_sum(block_low)
    expand_low = expand_back(right_outer(block_low, reduce_weight))[0].astype(jnp.bfloat16)
    expand_weight_grad = left_outer(normed_two_low, expand_low)
    expand_bias_grad = column_sum(expand_low)
    hidden_ln_grad, second_gain_grad, second_shift_grad = second_back(
        right_outer(expand_low, expand_weight)
    )
    hidden_grad = hidden_ln_grad + block_grad
    hidden_low = hidden_grad.astype(jnp.bfloat16)
    proj_weight_grad = left_outer(attended_low, hidden_low)
    proj_bias_grad = column_sum(hidden_low)
    out_grad_low = (
        right_outer(hidden_low, proj_weight)
        .astype(jnp.bfloat16)
        .reshape(slot_count, per_slot, head_count, HEAD)
    )
    row_delta = jnp.einsum("sqhd,sqhd->shq", out_grad_low.astype(jnp.float32), out_heads)
    pieces = (
        lax.all_gather(key_value, "blk", axis=2, tiled=True),
        lax.all_gather(keep_send, "blk", axis=2, tiled=True),
    )
    scores, allowed, key_rows, value_rows = scores_for(pieces)
    piece_width = pieces[0].shape[2]
    probs = jnp.where(allowed, jnp.exp(scores - log_total[..., None]), 0.0)
    prob_grad = jnp.einsum(
        "sqhd,skhd->shqk", out_grad_low, value_rows, preferred_element_type=jnp.float32
    )
    score_grad = (probs * (prob_grad - row_delta[..., None])).astype(jnp.bfloat16)
    query_grad = jnp.einsum(
        "shqk,skhd->sqhd", score_grad, key_rows, preferred_element_type=jnp.float32
    )
    key_grad = jnp.einsum(
        "shqk,sqhd->skhd", score_grad, query_low, preferred_element_type=jnp.float32
    )
    value_grad = jnp.einsum(
        "shqk,sqhd->skhd",
        probs.astype(jnp.bfloat16),
        out_grad_low,
        preferred_element_type=jnp.float32,
    )
    piece_grad = jnp.stack([key_grad, value_grad], 2).reshape(
        slot_count, per_slot, piece_width, 2 * model_width
    )
    pair_grad = piece_grad
    query_grad, pair_grad = (query_grad, pair_grad)
    own_pair = (
        lax.psum_scatter(pair_grad.astype(jnp.bfloat16), "blk", scatter_dimension=2, tiled=True)
        .astype(jnp.float32)
        .reshape(row_count, 2 * model_width)
    )
    qkv_low = jnp.concatenate(
        [query_grad.reshape(row_count, model_width) * 0.125, own_pair], 1
    ).astype(jnp.bfloat16)
    qkv_weight_grad = left_outer(normed_low, qkv_low)
    input_grad, first_gain_grad, first_shift_grad = first_back(right_outer(qkv_low, qkv_weight))
    tokens_grad = (input_grad + hidden_grad).astype(jnp.bfloat16).reshape(tokens.shape)
    (
        first_gain_grad,
        first_shift_grad,
        qkv_weight_grad,
        proj_weight_grad,
        proj_bias_grad,
        second_gain_grad,
        second_shift_grad,
        expand_weight_grad,
        expand_bias_grad,
        reduce_weight_grad,
        reduce_bias_grad,
        score_gain_grad,
        score_shift_grad,
        score_weight_grad,
        score_bias_grad,
        pred_weight_grad,
        pred_bias_grad,
        mid_weight_grad,
        mid_bias_grad,
        last_weight_grad,
        last_bias_grad,
    ) = lax.psum(
        (
            first_gain_grad,
            first_shift_grad,
            qkv_weight_grad,
            proj_weight_grad,
            proj_bias_grad,
            second_gain_grad,
            second_shift_grad,
            expand_weight_grad,
            expand_bias_grad,
            reduce_weight_grad,
            reduce_bias_grad,
            score_gain_grad,
            score_shift_grad,
            score_weight_grad,
            score_bias_grad,
            pred_weight_grad,
            pred_bias_grad,
            mid_weight_grad,
            mid_bias_grad,
            last_weight_grad,
            last_bias_grad,
        ),
        ("img", "blk"),
    )
    return (
        out_tokens,
        keep_prob,
        tokens_grad,
        first_gain_grad,
        first_shift_grad,
        qkv_weight_grad,
        proj_weight_grad,
        proj_bias_grad,
        second_gain_grad,
        second_shift_grad,
        expand_weight_grad,
        expand_bias_grad,
        reduce_weight_grad,
        reduce_bias_grad,
        score_gain_grad,
        score_shift_grad,
        score_weight_grad,
        score_bias_grad,
        pred_weight_grad,
        pred_bias_grad,
        mid_weight_grad,
        mid_bias_grad,
        last_weight_grad,
        last_bias_grad,
    )


LONGEST = 325
CHUNK = 32
ROWS = 256
BF = jnp.bfloat16
F32 = jnp.float32


def dot(a, b):
    return lax.dot_general(a, b, (((1,), (0,)), ((), ())), preferred_element_type=F32)


def dot_nt(a, b):
    return lax.dot_general(a, b, (((1,), (1,)), ((), ())), preferred_element_type=F32)


def dot_tn(a, b):
    return lax.dot_general(a, b, (((0,), (0,)), ((), ())), preferred_element_type=F32)


def split_two(v):
    high = v.astype(BF)
    return high, (v - high.astype(F32)).astype(BF)


def gelu_pair(v):
    phi = 0.5 * (1.0 + lax.erf(v * math.sqrt(0.5)))
    density = jnp.exp(v * v * -0.5) * (1.0 / math.sqrt(2.0 * math.pi))
    return v * phi, phi + v * density


def normalise(v):
    centre = v - jnp.mean(v, -1, keepdims=True)
    spread = jnp.mean(centre * centre, -1, keepdims=True)
    scale = lax.rsqrt(spread + EPS)
    return centre * scale, scale


def norm_back(grad, unit, scale, gain):
    inner = grad * gain
    mean_one = jnp.mean(inner, -1, keepdims=True)
    mean_two = jnp.mean(inner * unit, -1, keepdims=True)
    return scale * (inner - mean_one - unit * mean_two)


def total_rows(v):
    return jnp.sum(v.astype(F32), 0, keepdims=True)


def lanes(width):
    return lax.broadcasted_iota(jnp.int32, (1, width), 1)


def features(v):
    high = v.astype(BF)
    rest = v - high.astype(F32)
    middle = rest.astype(BF)
    least = (rest - middle.astype(F32)).astype(BF)
    spot = lanes(v.shape[1]) % HEAD
    zero = jnp.zeros_like(high)
    return jnp.where(spot == 0, high, jnp.where(spot == 1, middle, jnp.where(spot == 2, least, zero)))


def window(first, last, length, tile):
    if length < 650:
        return 0, length
    low = 0 if first < LONGEST else max(LONGEST, first - LONGEST + 1)
    high = LONGEST if last <= LONGEST else min(length, last - 1 + LONGEST)
    return low // tile * tile, min(length, -(-high // tile) * tile)


class Place:
    def __init__(self, axis, length, ends):
        self.axis, self.length, self.ends = axis, length, ends
        self.tile = CHUNK * axis

    def places(self, rows):
        return rows // self.tile * self.tile + rows % CHUNK * self.axis + rows % self.tile // CHUNK

    def segments(self, places):
        total = jnp.zeros_like(places)
        for end in self.ends:
            total += (places >= end).astype(jnp.int32)
        return total

    def column(self, start, count):
        rows = start + lax.broadcasted_iota(jnp.int32, (count, 1), 0)
        return self.places(rows)

    def row(self, start, count):
        rows = start + lax.broadcasted_iota(jnp.int32, (1, count), 1)
        return self.places(rows)


VEC = SimpleNamespace(
    first_gain=0, first_shift=1, proj_bias=2, second_gain=3, second_shift=4, expand_bias=5, reduce_bias=9,
    score_gain=10, score_shift=11, score_bias=12, pred_bias=13, mid_bias=14, last_weight=15, last_bias=16,
    query_sum=17, key_sum=18, value_sum=19,
)
VEC_ROWS = 32
MESH = pl.DeviceIdType.MESH
VMEM = pltpu.VMEM
DMA = pltpu.SemaphoreType.DMA


def names_of(**named):
    return tuple(named)


WEIGHTS = names_of(
    first_gain=0, first_shift=0, qkv_weight=0, proj_weight=0, proj_bias=0, second_gain=0, second_shift=0,
    expand_weight=0, expand_bias=0, reduce_weight=0, reduce_bias=0, score_gain=0, score_shift=0, score_weight=0,
    score_bias=0, pred_weight=0, pred_bias=0, mid_weight=0, mid_bias=0, last_weight=0, last_bias=0,
)
LARGE = names_of(
    qkv_weight=0, proj_weight=0, expand_weight=0, reduce_weight=0, score_weight=0, pred_weight=0, mid_weight=0
)
LAST_BIAS = WEIGHTS[-1]
LOADED = LARGE + tuple(n for n in WEIGHTS if n not in LARGE and n != LAST_BIAS)
SUMS = 7
PARTS = 4


class Sizes:
    def __init__(self, axis, groups, width, model, hidden, mid, images):
        self.axis, self.groups, self.width, self.model = axis, groups, width, model
        self.hidden, self.mid, self.images = hidden, mid, images
        self.length = axis * width
        self.tile = CHUNK * axis
        self.tiles = self.length // self.tile
        self.pairs = model // 128
        self.far = groups // 2
        step = 8 * self.far * 16
        self.filled = [0] * SUMS
        wide = model * self.pairs
        self.at = SimpleNamespace(
            score=self.reserve(0, wide), pred=self.reserve(0, model // 2 * self.pairs), mid=self.reserve(0, model // 2),
            reduce=self.reserve(1, hidden * self.pairs), expand=self.reserve(2, model * (hidden // 128)),
            proj=self.reserve(3, wide),
            qkv=[self.reserve(3 + min(p, 2), 3 * model) for p in range(self.pairs)],
            vec=self.reserve(6, VEC_ROWS * self.pairs),
        )
        self.kinds = [BF] * (SUMS - 1) + [F32]
        steps = [step] * (SUMS - 1) + [step // 2]
        self.rows = [-(-rows // each) * each for rows, each in zip(self.filled, steps)]
        self.windows = [window(i, i + ROWS, self.length, self.tile) for i in range(0, self.length, ROWS)]

    def reserve(self, group, rows):
        self.filled[group] += rows
        return group, self.filled[group] - rows


class Links:
    def __init__(self, far, send, receive):
        img, blk = lax.axis_index("img"), lax.axis_index("blk")
        self.far = far
        self.z, self.y, self.x, self.c = img // 2, img % 2, blk // 2, blk % 2
        self.send, self.receive, self.used, self.started = send, receive, 0, []

    def device(self, z, y, x, c):
        return (z * 2 + y, x * 2 + c)

    def mate(self):
        return self.device(self.z, self.y, self.x, 1 - self.c)

    def along(self, turn):
        return self.device(self.z, (self.y + turn) % 2, (self.x + 1 - turn) % 2, self.c)

    def level(self, k):
        return self.device((self.z + k) % self.far, self.y, self.x, self.c)

    def block(self, k):
        x, c = (self.x + k // 2) % 2, (self.c + k % 2) % 2
        return self.device(self.z, self.y, x, c), x * 2 + c

    def copy(self, source, target, device):
        i = self.used
        self.used += 1
        made = pltpu.make_async_remote_copy(
            src_ref=source, dst_ref=target, send_sem=self.send.at[i], recv_sem=self.receive.at[i],
            device_id=device, device_id_type=MESH,
        )
        made.start()
        self.started.append(made)
        return made

    def enter(self, meanwhile):
        barrier = pltpu.get_barrier_semaphore()
        partners = [self.block(k)[0] for k in (1, 2, 3)] + [self.along(1)]
        partners += [self.level(k) for k in range(1, self.far)]
        for partner in partners:
            pl.semaphore_signal(barrier, inc=1, device_id=partner, device_id_type=MESH)
        meanwhile()
        pl.semaphore_wait(barrier, len(partners))

    def finish(self):
        for made in self.started:
            made.wait_send()


def add_rows(target, start, other, other_start, count, step):
    def one(i, _):
        a = pl.ds(pl.multiple_of(start + i * step, 8), step)
        b = pl.ds(pl.multiple_of(other_start + i * step, 8), step)
        target[a, :] = (target[a, :].astype(F32) + other[b, :].astype(F32)).astype(target.dtype)
        return 0

    lax.fori_loop(0, count // step, one, 0)


class Level:
    def __init__(self, links, turn, flat, deep):
        self.links, self.turn, self.flat = links, turn, flat
        self.deep = links.far if deep else 1
        self.size = flat * self.deep

    def place(self, x, y, z):
        if self.flat == 1:
            at = 0
        elif self.turn is None:
            at = x * 2 + y
        else:
            at = x * (1 - self.turn) + y * self.turn
        return at * self.deep + (z if self.deep > 1 else 0)

    def mine(self):
        return self.place(self.links.x, self.links.y, self.links.z)

    def partner(self, k, back=1):
        t = self.links
        flat, z = k // self.deep, (t.z + back * (k % self.deep) + t.far) % t.far
        if self.flat == 1:
            x, y = t.x, t.y
        elif self.turn is None:
            x, y = (t.x + flat // 2) % 2, (t.y + flat % 2) % 2
        else:
            x, y = (t.x + (1 - self.turn) * flat) % 2, (t.y + self.turn * flat) % 2
        return t.device(z, y, x, t.c), self.place(x, y, z)


def levels_of(links, kind, core):
    both, deep = Level(links, None, 4, False), Level(links, 0, 1, True)
    x, y = Level(links, 0, 2, False), Level(links, 1, 2, False)
    if kind == TURNS:
        return [Level(links, core, 2, False), Level(links, 1 - core, 2, False), deep]
    return {FLAT: [both, deep], Y_FIRST: [y, x, deep], ALL: [Level(links, None, 4, True)], Y_DEEP: [y, deep, x]}[kind]


TURNS, FLAT, Y_FIRST, ALL, Y_DEEP = range(5)


def sum_group(links, kind, rows, buf, out, mate_in, level_in, own, own_sem):
    c = links.c
    levels = levels_of(links, kind, c)
    first_of_mate = levels_of(links, kind, 1 - c)[0]
    mate = links.mate()
    half = rows // 2
    n = half // (4 * links.far)

    def part(ref, start, size):
        return ref.at[pl.ds(pl.multiple_of(start, 8), size), :]

    def ordered(level, core_level):
        k = level.size
        return [core_level.partner(j)[1] for j in range(1, k)] + [core_level.mine()]

    base, size = c * half, half
    cut = levels[0].size if levels[0].size <= 4 else 1
    sub = half // cut
    pending = []
    to_mate = ordered(levels[0], first_of_mate) if cut > 1 else [0]
    for at in to_mate:
        pending.append([(links.copy(part(buf, (1 - c) * half + at * sub, sub), part(mate_in, at * sub, sub), mate), mate_in)])
    where = ordered(levels[0], levels[0]) if cut > 1 else [0]
    recv_at = 0
    for i, level in enumerate(levels):
        yield
        step = size // level.size
        following = levels[i + 1] if i + 1 < len(levels) else None
        split = level.size == 2 and following is not None and following.size == 2
        sent = [[], []] if split else [[]]
        spots = [level.partner(k)[1] for k in range(1, level.size)]

        def send(k):
            device, at = level.partner(k)
            slot = recv_at + (k - 1) * step
            if split:
                half_step = step // 2
                for j, two in enumerate((1 - following.mine(), following.mine())):
                    sent[j].append((links.copy(
                        part(buf, base + at * step + two * half_step, half_step),
                        part(level_in, slot + two * half_step, half_step), device), level_in, slot + two * half_step))
            else:
                sent[0].append((links.copy(part(buf, base + at * step, step), part(level_in, slot, step), device), level_in, slot))

        def take(group, at, count, first_in):
            for made in group:
                made[0].wait_recv()
                start = made[2] if len(made) > 2 else first_in
                add_rows(buf, base + at * count, made[1], start, count, min(count, 8 * n))

        if len(pending) == level.size:
            for k, (group, at) in enumerate(zip(pending, where), 1):
                take(group, at, step, at * step)
                if k < level.size:
                    send(k)
        else:
            for group in pending:
                take(group, 0, size, 0)
            for k in range(1, level.size):
                send(k)
        recv_at += (level.size - 1) * step
        base, size = base + level.mine() * step, step
        pending = sent
        where = [1 - following.mine(), following.mine()] if split else [0]
    yield
    total = buf[pl.ds(pl.multiple_of(base, 8), n), :].astype(F32)
    for made, ref, slot in pending[0]:
        made.wait_recv()
        total += ref[pl.ds(pl.multiple_of(slot, 8), n), :].astype(F32)
    own[...] = total.astype(own.dtype)
    at = part(out, base, n)
    local = pltpu.make_async_copy(own, at, own_sem)
    local.start()
    inner = levels[-1]
    back = [links.copy(own, at, inner.partner(k)[0]) for k in range(1, inner.size)]
    yield
    for made in back:
        made.wait_recv()
    local.wait()
    piece = n * inner.size
    base = base - inner.mine() * n
    outer = levels[:-1]
    flying = [[] for _ in outer]
    to_mate = []

    def pass_on(start, level_count):
        whole = part(out, start, piece)
        for i in reversed(range(level_count)):
            for k in range(1, outer[i].size):
                flying[i].append((k, links.copy(whole, whole, outer[i].partner(k)[0]), start))
        to_mate.append(links.copy(whole, whole, mate))

    pass_on(base, len(outer))
    step = piece
    for i in reversed(range(len(outer))):
        yield
        level = outer[i]
        for k, made, start in list(flying[i]):
            made.wait_recv()
            pass_on(start + (level.partner(k, -1)[1] - level.mine()) * step, i)
        step *= level.size
    yield
    for made in to_mate:
        made.wait_recv()


def layer_kernel(z, names, *refs):
    r = SimpleNamespace(**dict(zip(names, refs)))
    length, model, axis, pairs = z.length, z.model, z.axis, z.pairs
    tile, width = z.tile, z.width
    chunks = z.hidden // model
    links = Links(z.far, r.send, r.receive)
    mine = links.x * 2 + links.c
    local_used = [0]

    def local_copy(source, target):
        i = local_used[0]
        local_used[0] += 1
        made = pltpu.make_async_copy(source, target, r.load.at[i])
        made.start()
        return made

    small_loads = [
        local_copy(source, target)
        for source, target in ((r.keep_in, r.keep_in_v), (r.noise, r.noise_v), (r.grad_keep, r.grad_keep_v))
    ]
    w = SimpleNamespace(**{n: getattr(r, n + VALUE) for n in LOADED})
    given = w
    small_send, small = r.small_send, r.small

    def collect():
        for made in small_loads:
            made.wait()
        for s in range(axis):
            small_send[s, 0:1, :] = r.keep_in_v[s].astype(F32)
            small_send[s, 1:3, :] = r.noise_v[s]
            small_send[s, 3:4, :] = r.grad_keep_v[s]
            small_send[s, 4:8, :] = jnp.zeros((4, width), F32)

    links.enter(collect)

    halves = [slice(h * z.tiles // 2, (h + 1) * z.tiles // 2) for h in range(2)]

    def spread(source, target, part):
        return [
            links.copy(source.at[links.block(k)[1], part], target.at[part, mine], links.block(k)[0]) for k in (2, 3, 1)
        ]

    small_copies = [links.copy(small_send.at[links.block(k)[1]], small.at[mine], links.block(k)[0]) for k in (2, 3, 1)]
    token_copies = [spread(r.tokens, r.tok, part) for part in halves]
    loads = {n: local_copy(getattr(r, n), getattr(r, n + VALUE)) for n in LOADED}
    token_local = local_copy(r.tokens.at[mine], r.tok.at[:, mine])
    grad_local = local_copy(r.grad_out.at[mine], r.gout.at[:, mine])
    small[mine] = small_send[mine]

    ends = []
    total = 0
    for i in range(z.images):
        total = total + r.lengths[mine, i]
        ends.append(total)
    place = Place(axis, length, ends)

    meta, kept_row, vec = r.meta, r.kept_row, r.vec
    vec[...] = jnp.zeros_like(vec)
    groups = [r.buf0, r.buf1, r.buf2, r.buf3, r.buf4, r.buf5, r.buf6]
    for g in range(SUMS):
        if z.filled[g] < z.rows[g]:
            groups[g][z.filled[g] :, :] = jnp.zeros((z.rows[g] - z.filled[g], 128), z.kinds[g])
    for made in small_copies:
        made.wait_recv()
    for p in range(axis):
        block = jnp.concatenate([small[p], jnp.zeros((120, width), F32)], 0).T
        for t in range(z.tiles):
            meta[t * tile + p * CHUNK : t * tile + (p + 1) * CHUNK, :] = block[t * CHUNK : (t + 1) * CHUNK, :]
    for t in range(length // 128):
        kept_row[:, t * 128 : (t + 1) * 128] = meta[t * 128 : (t + 1) * 128, :].T[0:8]

    bias = [r.bias0, r.bias1, r.bias2, r.bias3]
    for i, (low, high) in enumerate(z.windows):
        spot_q, spot_k = place.column(i * ROWS, ROWS), place.row(low, high - low)
        segment_k = jnp.where((kept_row[0:1, low:high] > 0) & (spot_k < ends[-1]), place.segments(spot_k), -1)
        allowed = (place.segments(spot_q) == segment_k) | (spot_q == spot_k)
        bias[i][...] = jnp.where(allowed, 0.0, NEG)

    def vec_set(at, value):
        vec[at : at + 1, : value.shape[1]] = value

    def put(where, value, rows=0):
        group, at = where
        value = value.astype(z.kinds[group])
        for j in range(value.shape[1] // 128):
            groups[group][at + rows : at + rows + value.shape[0], :] = value[:, j * 128 : (j + 1) * 128]
            rows += value.shape[0]

    def row(ref):
        return ref[...].reshape(1, -1)

    def flat(ref):
        return ref[...].reshape(length, model)

    def tiled(ref, value):
        ref[...] = value.reshape(z.tiles, axis, CHUNK, model)

    spot = place.column(0, length)
    segment = place.segments(spot)
    live = (spot < ends[-1]).astype(F32)
    kept = jnp.where(meta[:, 0:1] > 0, live, 0.0)
    member = (segment == lanes(128)).astype(F32)
    r.member[...] = member.astype(BF)
    r.chosen[...] = (member * kept).astype(BF)

    for n in (LARGE[0], WEIGHTS[0], WEIGHTS[1]):
        loads.pop(n).wait()
    for t in (1, 2):
        r.weight_turned[t - 1] = w.qkv_weight[:, t * model : (t + 1) * model].T
    token_local.wait()
    half = lanes(128) < HEAD

    def project(h):
        rows = slice(h * length // 2, (h + 1) * length // 2)
        unit, _s = normalise(r.tok[halves[h]].reshape(length // 2, model).astype(F32))
        r.unit_low[rows, :] = unit.astype(BF)
        low = (unit * row(given.first_gain) + row(given.first_shift)).astype(BF)
        r.query[rows, :] = (dot(low, w.qkv_weight[:, :model]) * 0.125).astype(BF)
        key = dot(low, w.qkv_weight[:, model : 2 * model]).astype(BF)
        value = dot(low, w.qkv_weight[:, 2 * model :]).astype(BF)
        ones = jnp.ones((length // 2, 128), BF)
        for p in range(pairs):
            for ref, kind in ((r.key_ones, key), (r.value_ones, value)):
                ref[rows, p * 256 : p * 256 + 128] = kind[:, p * 128 : (p + 1) * 128]
                ref[rows, p * 256 + 128 : (p + 1) * 256] = ones

    def attend(i):
        low, high = z.windows[i]
        rows = slice(i * ROWS, (i + 1) * ROWS)
        for p in range(pairs):
            at = slice(p * 128, (p + 1) * 128)
            q = r.query[rows, at]
            outs, logs = [], []
            for side in (half, ~half):
                masked = jnp.where(side, q, jnp.zeros_like(q))
                scores = dot_nt(masked, r.key_ones[low:high, p * 256 : p * 256 + 128]) + bias[i][...]
                top = jnp.max(scores, -1, keepdims=True)
                weights = jnp.exp(scores - top).astype(BF)
                both = dot(weights, r.value_ones[low:high, p * 256 : (p + 1) * 256])
                outs.append(both[:, :128] / both[:, 128:])
                logs.append(top + jnp.log(both[:, 128:]))
            r.heads_out[rows, at] = jnp.where(half, outs[0], outs[1])
            r.lse_parts[rows, at] = features(-jnp.where(half, logs[0], logs[1]))

    early = [i for i, (_, high) in enumerate(z.windows) if max(high, (i + 1) * ROWS) <= length // 2]
    for h in range(2):
        for made in token_copies[h]:
            made.wait_recv()
        project(h)
        for i in range(len(z.windows)):
            if (i in early) == (h == 0):
                attend(i)
        if h == 0:
            grad_copies = spread(r.grad_out, r.gout, slice(0, z.tiles))

    for made in loads.values():
        made.wait()

    low = r.heads_out[...].astype(BF)
    r.attended[...] = low
    hid = flat(r.tok).astype(F32) + dot(low, w.proj_weight[...]) + row(given.proj_bias)
    r.hidden[...] = hid
    unit, _s = normalise(hid)
    low = (unit * row(given.second_gain) + row(given.second_shift)).astype(BF)
    r.normed_two[...] = low
    expand_bias = row(given.expand_bias)
    for c in range(chunks):
        at = slice(c * model, (c + 1) * model)
        act, slope = gelu_pair(dot(low, w.expand_weight[:, at]) + expand_bias[:, at])
        r.active[:, at] = act.astype(BF)
        r.expand_low[:, at] = slope.astype(BF)
    blk = hid + dot(r.active[...], w.reduce_weight[...]) + row(given.reduce_bias)
    r.block[...] = blk
    tiled(r.out_v, (blk * live).astype(BF))
    unit, _s = normalise(blk)
    low = (unit * row(given.score_gain) + row(given.score_shift)).astype(BF)
    r.score_in[...] = low
    act, slope = gelu_pair(dot(low, w.score_weight[...]) + row(given.score_bias))
    r.score_act[...] = act
    r.score_slope[...] = slope

    returned, locals_left = [], []

    def give_back(source, target):
        locals_left.append(local_copy(source.at[:, mine], target.at[mine]))
        for k in (2, 3, 1):
            device, at = links.block(k)
            returned.append(links.copy(source.at[:, at], target.at[mine], device))

    give_back(r.out_v, r.out_tokens)

    sums = dot_tn(r.chosen[...], act.astype(BF))
    counts = dot_tn(r.chosen[...], jnp.ones((length, 128), BF))
    inverse = jnp.tile(1.0 / jnp.maximum(counts, 1.0), (1, pairs))
    means = (sums * inverse).astype(BF)
    local_columns = lanes(model) < model // 2
    weight_gap = w.last_weight[0:1, :].astype(F32) - w.last_weight[1:2, :].astype(F32)
    bias_gap = r.last_bias[0] - r.last_bias[1]

    spread_mean = dot(r.member[...], means)
    join = jnp.where(local_columns, r.score_act[...], spread_mean).astype(BF)
    r.joined[...] = join
    act, pred_slope = gelu_pair(dot_nt(join, w.pred_weight[...]) + row(given.pred_bias))
    pred_low = act.astype(BF)
    r.pred_act[...] = pred_low
    act, mid_slope = gelu_pair(dot(pred_low, w.mid_weight[...]) + row(given.mid_bias))
    mid_low = act.astype(BF).astype(F32)
    info = meta[...]
    margin = jnp.sum(mid_low * weight_gap, -1, keepdims=True) + bias_gap + info[:, 1:2] - info[:, 2:3]
    sig = 1.0 / (1.0 + jnp.exp(-margin))
    r.keep_col[...] = jnp.broadcast_to(sig * kept, (length, 128))
    margin_grad = info[:, 3:4] * kept * sig * (1.0 - sig)
    vec_set(VEC.last_weight, jnp.sum(mid_low * margin_grad, 0, keepdims=True))
    vec_set(VEC.last_bias, jnp.sum(jnp.broadcast_to(margin_grad, (length, 128)), 0, keepdims=True))
    mid_grad = (margin_grad * weight_gap * mid_slope).astype(BF)
    r.mid_grad_low[...] = mid_grad
    vec_set(VEC.mid_bias, total_rows(mid_grad))
    pred_grad = (dot_nt(mid_grad, w.mid_weight[...]) * pred_slope).astype(BF)
    r.pred_grad_low[...] = pred_grad
    vec_set(VEC.pred_bias, total_rows(pred_grad))
    join_grad = dot(pred_grad, w.pred_weight[...])
    r.score_act[...] = join_grad
    mean_grad = (dot_tn(r.member[...], join_grad.astype(BF)) * inverse).astype(BF)

    def summing(g, names):
        return sum_group(links, KINDS[g], z.rows[g], *[getattr(r, n + str(g)) for n in names], r.own_sem.at[g])

    sum_names = names_of(buf=0, sum=0, mate_in=0, level_in=0, own=0)
    running = [summing(g, sum_names) for g in range(SUMS)]

    def advance(*which):
        for g in which:
            next(running[g], None)

    def point(i):
        advance(*PLAN.get(i, ()))

    spread_grad = dot(r.chosen[...], mean_grad)
    low = (jnp.where(local_columns, r.score_act[...], spread_grad) * r.score_slope[...]).astype(BF)
    r.score_grad_low[...] = low
    vec_set(VEC.score_bias, total_rows(low))
    grad_local.wait()
    for made in grad_copies:
        made.wait_recv()
    grad = dot_nt(r.score_grad_low[...], w.score_weight[...])
    unit, scale = normalise(r.block[...])
    vec_set(VEC.score_gain, jnp.sum(grad * unit, 0, keepdims=True))
    vec_set(VEC.score_shift, jnp.sum(grad, 0, keepdims=True))
    blk_grad = norm_back(grad, unit, scale, row(given.score_gain)) + flat(r.gout).astype(F32) * live
    r.block[...] = blk_grad
    low = blk_grad.astype(BF)
    r.block_low[...] = low
    vec_set(VEC.reduce_bias, total_rows(low))
    point(0)
    for c in range(chunks):
        part = dot_tn(r.active[:, c * model : (c + 1) * model], r.block_low[...]).astype(BF)
        for j in range(pairs):
            put(z.at.reduce, part[:, j * 128 : (j + 1) * 128], j * z.hidden + c * model)
        point(30 + c)
    advance(1)
    point(1)
    for c in range(chunks):
        at = slice(c * model, (c + 1) * model)
        piece = (dot_nt(r.block_low[...], w.reduce_weight[at, :]) * r.expand_low[:, at].astype(F32)).astype(BF)
        r.expand_low[:, at] = piece
        vec_set(VEC.expand_bias + c, total_rows(piece))
        put(z.at.expand, dot_tn(r.normed_two[...], piece), c * pairs * model)
        if c + 1 == chunks:
            advance(2)
        point(2 + c)

    put(z.at.score, dot_tn(r.score_in[...], r.score_grad_low[...]))
    put(z.at.pred, dot_tn(r.pred_grad_low[...], r.joined[...]))
    mid = dot_tn(r.pred_act[...], r.mid_grad_low[...])
    put(z.at.mid, jnp.concatenate([mid, jnp.zeros((model // 2, 128 - z.mid), F32)], 1))
    advance(0)

    for p in range(axis):
        parts = [r.keep_col[t * tile + p * CHUNK : t * tile + (p + 1) * CHUNK, :] for t in range(z.tiles)]
        r.keep_v[p] = jnp.concatenate(parts, 0).T[0:8]
    for k in (2, 3, 1):
        device, at = links.block(k)
        returned.append(links.copy(r.keep_v.at[at], r.keep.at[mine], device))
    locals_left.append(local_copy(r.keep_v.at[mine], r.keep.at[mine]))

    grad = dot_nt(r.expand_low[...], w.expand_weight[...])
    unit, scale = normalise(r.hidden[...])
    vec_set(VEC.second_gain, jnp.sum(grad * unit, 0, keepdims=True))
    vec_set(VEC.second_shift, jnp.sum(grad, 0, keepdims=True))
    hid_grad = norm_back(grad, unit, scale, row(given.second_gain)) + r.block[...]
    r.hidden[...] = hid_grad
    low = hid_grad.astype(BF)
    r.hidden_low[...] = low
    vec_set(VEC.proj_bias, total_rows(low))
    point(40)
    low = dot_nt(low, w.proj_weight[...]).astype(BF)
    r.attended_grad[...] = low
    one, two = split_two(low.astype(F32) * r.heads_out[...])
    pair_sum = (
        lax.broadcasted_iota(jnp.int32, (128, 128), 0) // HEAD == lax.broadcasted_iota(jnp.int32, (128, 128), 1) // HEAD
    ).astype(BF)
    for p in range(pairs):
        at = slice(p * 128, (p + 1) * 128)
        r.delta_parts[:, at] = features(-(dot(one[:, at], pair_sum) + dot(two[:, at], pair_sum)))
    r.query_turned[...] = r.query[...].T
    point(6)
    put(z.at.proj, dot_tn(r.attended[...], r.hidden_low[...]))
    point(7)
    r.attended_turned[...] = r.attended_grad[...].T

    r.key_turned[...] = jnp.zeros((model, length), F32)
    r.value_turned[...] = jnp.zeros((model, length), F32)
    unit_count = 0
    for p in range(pairs):
        at = slice(p * 128, (p + 1) * 128)
        wide = slice(p * 256, (p + 1) * 256)
        near = slice(p * 256, p * 256 + 128)
        for i, (low, high) in enumerate(z.windows):
            rows = slice(i * ROWS, (i + 1) * ROWS)
            q, lse, og, delta = r.query[rows, at], r.lse_parts[rows, at], r.attended_grad[rows, at], r.delta_parts[rows, at]
            zero = jnp.zeros_like(q)
            query_parts = []
            for h, side in enumerate((half, ~half)):
                head = slice((2 * p + h) * HEAD, (2 * p + h + 1) * HEAD)
                wide_q = jnp.concatenate([jnp.where(side, q, zero), jnp.where(side, lse, zero)], 1)
                wide_o = jnp.concatenate([jnp.where(side, og, zero), jnp.where(side, delta, zero)], 1)
                probs = jnp.exp(dot_nt(wide_q, r.key_ones[low:high, wide]) + bias[i][...])
                score_grad = (probs * dot_nt(wide_o, r.value_ones[low:high, wide])).astype(BF)
                r.value_turned[head, low:high] += dot(r.attended_turned[head, rows], probs.astype(BF))
                r.key_turned[head, low:high] += dot(r.query_turned[head, rows], score_grad)
                query_parts.append(dot(score_grad, r.key_ones[low:high, near]))
            r.query_grad[rows, at] = (jnp.where(half, query_parts[0], query_parts[1]) * 0.125).astype(BF)
            point(8 + unit_count)
            unit_count += 1
        part = r.query_grad[:, at]
        put(z.at.qkv[p], dot_tn(r.unit_low[...], part))
        vec[VEC.query_sum : VEC.query_sum + 1, at] = total_rows(part)
        for t, (ref, name) in enumerate(((r.key_turned, VEC.key_sum), (r.value_turned, VEC.value_sum)), 1):
            part = ref[at, :].astype(BF)
            r.turned_low[t - 1, at, :] = part
            put(z.at.qkv[p], dot(part, r.unit_low[...]), t * model)
            vec[name : name + 1, at] = dot_nt(jnp.ones((8, length), BF), part)[0:1]
        advance(z.at.qkv[p][0])
    put(z.at.vec, vec[...])
    advance(6)
    point(20)

    grad = dot_nt(r.query_grad[...], w.qkv_weight[:, :model])
    for t in range(2):
        grad += dot_tn(r.turned_low[t], r.weight_turned[t])
    point(41)
    unit, scale = normalise(flat(r.tok).astype(F32))
    tiled(r.grad_v, (norm_back(grad, unit, scale, row(given.first_gain)) + r.hidden[...]).astype(BF))
    locals_left.append(local_copy(r.grad_v.at[:, mine], r.tokens_grad.at[mine]))

    def give_part(i):
        part = slice(i * z.tiles // PARTS, (i + 1) * z.tiles // PARTS)
        for k in (2, 3, 1):
            device, at = links.block(k)
            returned.append(links.copy(r.grad_v.at[part, at], r.tokens_grad.at[mine, part], device))

    point(21)
    given_parts = 0
    for g in PLAN_END + (SUMS,) * PARTS:
        if g < SUMS:
            advance(g)
        elif given_parts < PARTS:
            give_part(given_parts)
            given_parts += 1
    for _ in range(20):
        advance(*range(SUMS))
    for made in returned:
        made.wait_recv()
    for made in locals_left:
        made.wait()
    links.finish()


VALUE = "_v"
KINDS = (FLAT, TURNS, TURNS, TURNS, TURNS, TURNS, FLAT)
PLAN = {5: (1,), 40: (0,), 7: (2,), 10: (1,), 13: (3,), 14: (2,), 15: (1,), 16: (0,), 17: (3,), 19: (2, 4), 41: (6, 3, 5, 1)}
PLAN_END = (4, 0, 7, 5, 7, 7, 6, 4, 3, 5, 2, 1, 6, 0, 3, 5, 1, 4, 2, 3, 5, 1, 6, 4, 2, 5, 4, 1, 3, 6, 7, 3, 2, 5, 0, 4, 6, 5, 2, 0, 4)


def run_layer(z, tokens, grad_out, keep_in, noise, grad_keep, lengths, weights):
    L, D, U = z.length, z.model, z.hidden
    half = D // 2
    sm, far = (pl.BlockSpec(memory_space=m) for m in (pltpu.SMEM, pl.ANY))
    inputs = dict(
        tokens=(tokens, far), grad_out=(grad_out, far), keep_in=(keep_in, far), noise=(noise, far),
        grad_keep=(grad_keep, far), lengths=(lengths, sm),
    )
    for n in WEIGHTS:
        inputs[n] = (weights[n], sm if n == LAST_BIAS else far)
    four = jax.ShapeDtypeStruct((z.axis, z.tiles, CHUNK, D), BF)
    outs = dict(out_tokens=four, keep=jax.ShapeDtypeStruct((z.axis, 8, z.width), F32), tokens_grad=four)
    low = lambda *s: VMEM(s, BF)
    full = lambda *s: VMEM(s, F32)
    tiles = low(z.tiles, z.axis, CHUNK, D)
    small = full(z.axis, 8, z.width)
    scratch = dict(
        tok=tiles, gout=tiles, out_v=tiles, grad_v=tiles, small_send=small, small=small, keep_v=small,
        meta=full(L, 128), kept_row=full(8, L), member=low(L, 128), chosen=low(L, 128),
        unit_low=low(L, D), query=low(L, D), query_turned=low(D, L), attended_turned=low(D, L), key_turned=full(D, L),
        value_turned=full(D, L), turned_low=low(2, D, L), weight_turned=low(2, D, D), key_ones=low(L, 2 * D), value_ones=low(L, 2 * D),
        heads_out=full(L, D), lse_parts=low(L, D), delta_parts=low(L, D), attended=low(L, D),
        hidden=full(L, D), normed_two=low(L, D), active=low(L, U), expand_low=low(L, U),
        block=full(L, D), score_in=low(L, D), score_act=full(L, D), score_slope=full(L, D),
        joined=low(L, D), pred_act=low(L, half), mid_grad_low=low(L, z.mid), pred_grad_low=low(L, half),
        score_grad_low=low(L, D), block_low=low(L, D), hidden_low=low(L, D), attended_grad=low(L, D),
        query_grad=low(L, D), vec=full(VEC_ROWS, D), keep_col=full(L, 128),
    )
    for n in LOADED:
        scratch[n + VALUE] = VMEM(weights[n].shape, weights[n].dtype)
    scratch.update(keep_in_v=VMEM(keep_in.shape, jnp.int32), noise_v=full(*noise.shape), grad_keep_v=full(*grad_keep.shape))
    for i, (first, last) in enumerate(z.windows):
        scratch["bias%d" % i] = full(ROWS, last - first)
    sum_names = names_of(sum=0, buf=0, mate_in=0, level_in=0, own=0)
    for g, (rows, kind) in enumerate(zip(z.rows, z.kinds)):
        n = rows // (8 * z.far)
        shapes = [(rows, 128), (rows, 128), (rows // 2, 128), (rows // 2 - n, 128), (n, 128)]
        outs[sum_names[0] + str(g)] = jax.ShapeDtypeStruct(shapes[0], kind)
        scratch.update((name + str(g), VMEM(shape, kind)) for name, shape in zip(sum_names[1:], shapes[1:]))
    sems = 12 + 3 * PARTS + SUMS * 36
    scratch.update(send=DMA((sems,)), receive=DMA((sems,)), load=DMA((len(LOADED) + 8,)), own_sem=DMA((SUMS,)))
    results = pl.pallas_call(
        functools.partial(layer_kernel, z, tuple(inputs) + tuple(outs) + tuple(scratch)),
        out_shape=list(outs.values()),
        in_specs=[spec for _, spec in inputs.values()],
        out_specs=[far] * len(outs),
        scratch_shapes=list(scratch.values()),
        compiler_params=pltpu.CompilerParams(collective_id=0, has_side_effects=True, vmem_limit_bytes=63 * 2**20),
        name="layer",
    )(*[array for array, _ in inputs.values()])
    return dict(zip(outs, results))


STAGED = names_of(reduce_weight=0, score_weight=0, pred_weight=0, expand_weight=0, proj_weight=0, qkv_weight=0)
GIVEN = names_of(qkv_given=0, gain_given=0, shift_given=0)
PASSED = names_of(out_tokens=0, tokens_grad=0)


def unpack_kernel(z, names, *refs):
    r = SimpleNamespace(**dict(zip(names, refs)))
    out = SimpleNamespace(**{n: getattr(r, n + VALUE) if n in STAGED else getattr(r, n) for n in WEIGHTS})
    sums = [r.in0, r.in1, r.in2, r.in3, r.in4, r.in5, r.in6]
    used = [0]

    def start(source, target):
        made = pltpu.make_async_copy(source, target, r.sem.at[used[0]])
        used[0] += 1
        made.start()
        return made

    given = [start(r.qkv_given, r.weight), start(r.gain_given, r.gain), start(r.shift_given, r.shift)]
    loads = [start(source, ref) for source, ref in zip((r.sum0, r.sum1, r.sum2, r.sum3, r.sum4, r.sum5, r.sum6), sums)]
    through = [start(r.out_tokens, r.out_tokens_v), start(r.tokens_grad, r.tokens_grad_v)]
    stored = []
    model, pairs, half = z.model, z.pairs, z.model // 2

    def take(where, first, count):
        group, at = where
        return sums[group][at + first : at + first + count, :].astype(F32)

    def store(*names):
        stored.extend(start(getattr(r, n + VALUE), getattr(r, n)) for n in names)

    loads[0].wait()
    for j in range(pairs):
        at = slice(j * 128, (j + 1) * 128)
        out.score_weight[:, at] = take(z.at.score, j * model, model)
        out.pred_weight[:, at] = take(z.at.pred, j * half, half)
    out.mid_weight[...] = take(z.at.mid, 0, half)[:, : z.mid]
    store(STAGED[1], STAGED[2])
    loads[1].wait()
    for j in range(pairs):
        out.reduce_weight[:, j * 128 : (j + 1) * 128] = take(z.at.reduce, j * z.hidden, z.hidden)
    store(STAGED[0])
    loads[2].wait()
    for j in range(z.hidden // 128):
        out.expand_weight[:, j * 128 : (j + 1) * 128] = take(z.at.expand, j * model, model)
    store(STAGED[3])
    through[0].wait()
    through[1].wait()
    stored.append(start(r.out_tokens_v, r.out_tokens_out))
    stored.append(start(r.tokens_grad_v, r.tokens_grad_out))
    loads[3].wait()
    loads[4].wait()
    loads[5].wait()
    loads[6].wait()
    vec = jnp.concatenate([take(z.at.vec, j * VEC_ROWS, VEC_ROWS) for j in range(pairs)], 1)

    def row(at):
        return vec[at : at + 1, :]

    def turned(ref):
        return jnp.broadcast_to(ref[...].reshape(1, model), (128, model)).T

    for made in given:
        made.wait()
    gain, shift = turned(r.gain), turned(r.shift)
    gain_grad, shift_grad = jnp.zeros((model, 128), F32), jnp.zeros((model, 128), F32)
    for j in range(pairs):
        out.proj_weight[:, j * 128 : (j + 1) * 128] = take(z.at.proj, j * model, model)
        for t, name in enumerate((VEC.query_sum, VEC.key_sum, VEC.value_sum)):
            part = take(z.at.qkv[j], t * model, model)
            if t:
                part = jnp.concatenate([part[b * 128 : (b + 1) * 128, :].T for b in range(pairs)], 0)
            at = slice(t * model + j * 128, t * model + (j + 1) * 128)
            total = row(name)[:, j * 128 : (j + 1) * 128]
            weight = r.weight[:, at].astype(F32)
            out.qkv_weight[:, at] = gain * part + shift * total
            gain_grad += weight * part
            shift_grad += weight * total
    store(STAGED[4], STAGED[5])
    out.first_gain[...] = jnp.sum(gain_grad.T, 0, keepdims=True).reshape(model)
    out.first_shift[...] = jnp.sum(shift_grad.T, 0, keepdims=True).reshape(model)
    chunks = z.hidden // model
    for ref, at in (
        (out.proj_bias, VEC.proj_bias),
        (out.second_gain, VEC.second_gain), (out.second_shift, VEC.second_shift), (out.reduce_bias, VEC.reduce_bias),
        (out.score_gain, VEC.score_gain), (out.score_shift, VEC.score_shift), (out.score_bias, VEC.score_bias),
    ):
        ref[...] = row(at).reshape(model)
    out.expand_bias[...] = jnp.concatenate([row(VEC.expand_bias + c) for c in range(chunks)], 1).reshape(z.hidden)
    out.pred_bias[...] = row(VEC.pred_bias)[:, :half].reshape(half)
    out.mid_bias[...] = row(VEC.mid_bias)[:, : z.mid].reshape(z.mid)
    gap = row(VEC.last_weight)[:, : z.mid]
    out.last_weight[...] = jnp.concatenate([gap, -gap], 0)
    gap = row(VEC.last_bias)[:, 0:2]
    out.last_bias[...] = jnp.where(lanes(2) == 0, gap, -gap).reshape(2)
    for s in range(z.axis):
        r.keep_out[s] = r.keep[s, 0:1, :]
    for made in stored:
        made.wait()


def run_unpack(z, results, shapes, given):
    far, vm = pl.BlockSpec(memory_space=pl.ANY), pl.BlockSpec(memory_space=pltpu.VMEM)
    tokens = results[PASSED[0]]
    outs = dict(
        out_tokens_out=(tokens, far), keep_out=(jax.ShapeDtypeStruct((z.axis, 1, z.width), F32), vm),
        tokens_grad_out=(tokens, far),
    )
    for n in WEIGHTS:
        outs[n] = (jax.ShapeDtypeStruct(shapes[n], F32), far if n in STAGED else vm)
    scratch = dict(out_tokens_v=VMEM(tokens.shape, BF), tokens_grad_v=VMEM(tokens.shape, BF))
    for g in range(SUMS):
        scratch["in%d" % g] = VMEM((z.rows[g], 128), z.kinds[g])
    for n in STAGED:
        scratch[n + VALUE] = VMEM(shapes[n], F32)
    scratch.update(
        sem=DMA((SUMS + 7 + len(STAGED),)), weight=VMEM(given[0].shape, BF), gain=VMEM(given[1].shape, F32),
        shift=VMEM(given[2].shape, F32),
    )
    done = pl.pallas_call(
        functools.partial(unpack_kernel, z, tuple(results) + GIVEN + tuple(outs) + tuple(scratch)),
        out_shape=[jax.ShapeDtypeStruct(s.shape, s.dtype) for s, _ in outs.values()],
        in_specs=[far, vm] + [far] * (SUMS + 4),
        out_specs=[spec for _, spec in outs.values()],
        scratch_shapes=list(scratch.values()),
        compiler_params=pltpu.CompilerParams(vmem_limit_bytes=63 * 2**20),
        name="unpack",
    )(*results.values(), *given)
    return done


def per_device(tokens, lengths, keep_in, noise, *rest):
    weights, (grad_out, grad_keep) = dict(zip(WEIGHTS, rest[:21])), rest[21:]
    slots, width, _, model = tokens.shape
    w = SimpleNamespace(**weights)
    z = Sizes(
        slots, lax.axis_size("img"), width, model, w.expand_weight.shape[1], w.mid_weight.shape[1], lengths.shape[1]
    )
    turned = names_of(pred_weight=0, last_weight=0)
    for n in turned:
        weights[n] = weights[n].T
    four = (slots, width // CHUNK, CHUNK, model)
    results = run_layer(
        z, tokens.reshape(four), grad_out.reshape(four), keep_in.reshape(slots, 1, width),
        noise.reshape(slots, width, 2).swapaxes(1, 2), grad_keep.reshape(slots, 1, width), lengths, weights,
    )
    given = (w.qkv_weight, w.first_gain, w.first_shift)
    done = run_unpack(z, results, {n: v.shape for n, v in weights.items()}, given)
    back = dict(zip(WEIGHTS, done[3:]))
    for n in turned:
        back[n] = back[n].T
    return (
        done[0].reshape(tokens.shape), done[1].reshape(keep_in.shape), done[2].reshape(tokens.shape)
    ) + tuple(back.values())


def solution(mesh):
    split = P("img", None, "blk", None)
    placed = (split, P("img", None), P("img", None, "blk"), split) + (P(),) * 21 + (split, P("img", None, "blk"))

    def chosen_device(*arrays):
        return (per_device if arrays[0].shape[0] == mesh.shape["blk"] == 4 else general_device)(*arrays)

    return jax.shard_map(
        chosen_device, mesh=mesh, in_specs=placed, out_specs=(split, P("img", None, "blk"), split) + (P(),) * 21,
        check_vma=False,
    )
```

```python
import functools
import math
from types import SimpleNamespace

import jax
import jax.numpy as jnp
from jax import lax
from jax.experimental import pallas as pl
from jax.experimental.pallas import tpu as pltpu
from jax.sharding import PartitionSpec as P

HEAD = 64

EPS = 1e-06
NEG = -1e30
HIGH = lax.Precision.HIGHEST


def layer_norm(row_data, norm_gain, norm_shift):
    centre = row_data - jnp.mean(row_data, -1, keepdims=True)
    spread = jnp.mean(centre * centre, -1, keepdims=True)
    return centre * lax.rsqrt(spread + EPS) * norm_gain + norm_shift


def gelu_exact(values):
    return jax.nn.gelu(values, approximate=False)


def matmul(former, latter):
    return jnp.dot(former, latter, preferred_element_type=jnp.float32)


def left_outer(former, latter):
    return lax.dot_general(
        former, latter, (((0,), (0,)), ((), ())), preferred_element_type=jnp.float32
    )


def right_outer(former, latter):
    return lax.dot_general(
        former, latter, (((1,), (1,)), ((), ())), preferred_element_type=jnp.float32
    )


def column_sum(values):
    return jnp.sum(values.astype(jnp.float32), 0)


def general_device(
    tokens,
    lengths,
    keep_in,
    noise,
    first_gain,
    first_shift,
    qkv_weight,
    proj_weight,
    proj_bias,
    second_gain,
    second_shift,
    expand_weight,
    expand_bias,
    reduce_weight,
    reduce_bias,
    score_gain,
    score_shift,
    score_weight,
    score_bias,
    pred_weight,
    pred_bias,
    mid_weight,
    mid_bias,
    last_weight,
    last_bias,
    grad_out,
    grad_keep,
):
    slot_count, per_slot, _, model_width = tokens.shape
    row_count = slot_count * per_slot
    head_count = model_width // HEAD
    axis_count = lax.axis_size("blk")
    axis_place = lax.axis_index("blk")
    image_ends = jnp.cumsum(lengths, 1)
    totals = image_ends[:, -1:]
    image_count = lengths.shape[1]

    def locate(places):
        segment = jnp.sum((image_ends[:, None, :] <= places[None, :, None]).astype(jnp.int32), -1)
        return (segment, places[None, :] < totals)

    query_place = jnp.arange(per_slot, dtype=jnp.int32) * axis_count + axis_place
    query_segment, query_live = locate(query_place)
    kept_mask = (keep_in[:, :, 0] > 0) & query_live
    kept_float = kept_mask.astype(jnp.float32)
    live_float = query_live.astype(jnp.float32).reshape(row_count, 1)
    kept_rows = kept_float.reshape(row_count)
    row_data = tokens.reshape(row_count, model_width).astype(jnp.float32)
    normed, first_back = jax.vjp(layer_norm, row_data, first_gain, first_shift)
    normed_low = normed.astype(jnp.bfloat16)
    qkv_rows = matmul(normed_low, qkv_weight)
    query_low = (
        (qkv_rows[:, :model_width] * 0.125)
        .astype(jnp.bfloat16)
        .reshape(slot_count, per_slot, head_count, HEAD)
    )
    key_value = (
        qkv_rows[:, model_width:]
        .astype(jnp.bfloat16)
        .reshape(slot_count, per_slot, 1, 2 * model_width)
    )
    keep_send = keep_in.astype(jnp.bfloat16)

    def scores_for(pieces):
        key_piece, keep_piece = pieces
        piece_width = key_piece.shape[2]
        key_place = (
            jnp.arange(per_slot, dtype=jnp.int32)[:, None] * axis_count
            + jnp.arange(piece_width, dtype=jnp.int32)[None, :]
        ).reshape(per_slot * piece_width)
        key_segment, key_live = locate(key_place)
        key_kept = (keep_piece.reshape(slot_count, per_slot * piece_width) > 0) & key_live
        allowed = (query_segment[:, :, None] == key_segment[:, None, :]) & key_kept[:, None, :] | (
            query_place[:, None] == key_place[None, :]
        )[None]
        split_keys = key_piece.reshape(slot_count, per_slot * piece_width, 2, head_count, HEAD)
        key_rows = split_keys[:, :, 0]
        value_rows = split_keys[:, :, 1]
        scores = jnp.einsum(
            "sqhd,skhd->shqk", query_low, key_rows, preferred_element_type=jnp.float32
        )
        return (scores, allowed[:, None], key_rows, value_rows)

    run_max = jnp.full((slot_count, head_count, per_slot), NEG, jnp.float32)
    summed = jnp.zeros((slot_count, per_slot, head_count, HEAD), jnp.float32)
    scores, allowed, key_rows, value_rows = scores_for(
        (
            lax.all_gather(key_value, "blk", axis=2, tiled=True),
            lax.all_gather(keep_send, "blk", axis=2, tiled=True),
        )
    )
    scores = jnp.where(allowed, scores, NEG)
    new_max = jnp.maximum(run_max, jnp.max(scores, -1))
    weights = jnp.where(allowed, jnp.exp(scores - new_max[..., None]), 0.0)
    factor = jnp.exp(run_max - new_max)
    update = jnp.einsum(
        "shqk,skhd->sqhd",
        weights.astype(jnp.bfloat16),
        value_rows,
        preferred_element_type=jnp.float32,
    )
    summed = summed * jnp.swapaxes(factor, 1, 2)[..., None] + update
    run_max, run_sum, summed = (new_max, jnp.sum(weights, -1), summed)
    out_heads = summed / jnp.swapaxes(run_sum, 1, 2)[..., None]
    log_total = run_max + jnp.log(run_sum)
    attended_low = out_heads.reshape(row_count, model_width).astype(jnp.bfloat16)
    hidden = row_data + matmul(attended_low, proj_weight) + proj_bias
    normed_two, second_back = jax.vjp(layer_norm, hidden, second_gain, second_shift)
    normed_two_low = normed_two.astype(jnp.bfloat16)
    expand = matmul(normed_two_low, expand_weight) + expand_bias
    active, expand_back = jax.vjp(gelu_exact, expand)
    active_low = active.astype(jnp.bfloat16)
    block = hidden + matmul(active_low, reduce_weight) + reduce_bias
    out_tokens = (block * live_float).astype(jnp.bfloat16).reshape(tokens.shape)
    score_in, score_back = jax.vjp(layer_norm, block, score_gain, score_shift)
    score_low = score_in.astype(jnp.bfloat16)
    score_pre = matmul(score_low, score_weight) + score_bias
    score_act, score_gelu_back = jax.vjp(gelu_exact, score_pre)
    half_width = score_act.shape[1] // 2
    member = (
        query_segment[:, :, None] == jnp.arange(image_count, dtype=jnp.int32)[None, None, :]
    ).astype(jnp.float32)
    chosen = member * kept_float[..., None]
    global_part = score_act[:, half_width:].reshape(slot_count, per_slot, half_width)
    part_sums = jnp.einsum("sti,stc->sic", chosen, global_part, precision=HIGH)
    part_counts = jnp.sum(chosen, 1)
    image_sums, image_counts = (
        lax.psum(part_sums.astype(jnp.bfloat16), "blk").astype(jnp.float32),
        lax.psum(part_counts.astype(jnp.bfloat16), "blk").astype(jnp.float32),
    )
    inverse = 1.0 / jnp.maximum(image_counts, 1.0)
    image_means = image_sums * inverse[..., None]
    spread_mean = jnp.einsum("sti,sic->stc", member, image_means, precision=HIGH).reshape(
        row_count, half_width
    )
    joined_low = jnp.concatenate([score_act[:, :half_width], spread_mean], 1).astype(jnp.bfloat16)
    pred_pre = matmul(joined_low, pred_weight) + pred_bias
    pred_act, pred_gelu_back = jax.vjp(gelu_exact, pred_pre)
    pred_low = pred_act.astype(jnp.bfloat16)
    mid_pre = matmul(pred_low, mid_weight) + mid_bias
    mid_act, mid_gelu_back = jax.vjp(gelu_exact, mid_pre)
    mid_low = mid_act.astype(jnp.bfloat16)
    logits = matmul(mid_low, last_weight) + last_bias
    noise_rows = noise.reshape(row_count, 2)
    margin = logits[:, 0] - logits[:, 1] + noise_rows[:, 0] - noise_rows[:, 1]
    keep_sigmoid = jax.nn.sigmoid(margin)
    keep_prob = (keep_sigmoid * kept_rows).reshape(keep_in.shape)
    margin_grad = grad_keep.reshape(row_count) * kept_rows * keep_sigmoid * (1.0 - keep_sigmoid)
    logit_grad = jnp.stack([margin_grad, -margin_grad], 1)
    last_weight_grad = lax.dot_general(
        mid_low.astype(jnp.float32), logit_grad, (((0,), (0,)), ((), ())), precision=HIGH
    )
    last_bias_grad = jnp.sum(logit_grad, 0)
    mid_grad = lax.dot_general(
        logit_grad, last_weight.astype(jnp.float32), (((1,), (1,)), ((), ())), precision=HIGH
    )
    mid_pre_low = mid_gelu_back(mid_grad)[0].astype(jnp.bfloat16)
    mid_weight_grad = left_outer(pred_low, mid_pre_low)
    mid_bias_grad = column_sum(mid_pre_low)
    pred_pre_low = pred_gelu_back(right_outer(mid_pre_low, mid_weight))[0].astype(jnp.bfloat16)
    pred_weight_grad = left_outer(joined_low, pred_pre_low)
    pred_bias_grad = column_sum(pred_pre_low)
    joined_grad = right_outer(pred_pre_low, pred_weight)
    spread_grad = joined_grad[:, half_width:].reshape(slot_count, per_slot, half_width)
    part_mean_grad = jnp.einsum("sti,stc->sic", member, spread_grad, precision=HIGH)
    mean_grad = lax.psum(part_mean_grad.astype(jnp.bfloat16), "blk").astype(jnp.float32)
    global_grad = jnp.einsum(
        "sti,sic->stc", chosen, mean_grad * inverse[..., None], precision=HIGH
    ).reshape(row_count, half_width)
    act_grad = jnp.concatenate([joined_grad[:, :half_width], global_grad], 1)
    score_pre_low = score_gelu_back(act_grad)[0].astype(jnp.bfloat16)
    score_weight_grad = left_outer(score_low, score_pre_low)
    score_bias_grad = column_sum(score_pre_low)
    block_pred_grad, score_gain_grad, score_shift_grad = score_back(
        right_outer(score_pre_low, score_weight)
    )
    block_grad = (
        block_pred_grad + grad_out.reshape(row_count, model_width).astype(jnp.float32) * live_float
    )
    block_low = block_grad.astype(jnp.bfloat16)
    reduce_weight_grad = left_outer(active_low, block_low)
    reduce_bias_grad = column_sum(block_low)
    expand_low = expand_back(right_outer(block_low, reduce_weight))[0].astype(jnp.bfloat16)
    expand_weight_grad = left_outer(normed_two_low, expand_low)
    expand_bias_grad = column_sum(expand_low)
    hidden_ln_grad, second_gain_grad, second_shift_grad = second_back(
        right_outer(expand_low, expand_weight)
    )
    hidden_grad = hidden_ln_grad + block_grad
    hidden_low = hidden_grad.astype(jnp.bfloat16)
    proj_weight_grad = left_outer(attended_low, hidden_low)
    proj_bias_grad = column_sum(hidden_low)
    out_grad_low = (
        right_outer(hidden_low, proj_weight)
        .astype(jnp.bfloat16)
        .reshape(slot_count, per_slot, head_count, HEAD)
    )
    row_delta = jnp.einsum("sqhd,sqhd->shq", out_grad_low.astype(jnp.float32), out_heads)
    pieces = (
        lax.all_gather(key_value, "blk", axis=2, tiled=True),
        lax.all_gather(keep_send, "blk", axis=2, tiled=True),
    )
    scores, allowed, key_rows, value_rows = scores_for(pieces)
    piece_width = pieces[0].shape[2]
    probs = jnp.where(allowed, jnp.exp(scores - log_total[..., None]), 0.0)
    prob_grad = jnp.einsum(
        "sqhd,skhd->shqk", out_grad_low, value_rows, preferred_element_type=jnp.float32
    )
    score_grad = (probs * (prob_grad - row_delta[..., None])).astype(jnp.bfloat16)
    query_grad = jnp.einsum(
        "shqk,skhd->sqhd", score_grad, key_rows, preferred_element_type=jnp.float32
    )
    key_grad = jnp.einsum(
        "shqk,sqhd->skhd", score_grad, query_low, preferred_element_type=jnp.float32
    )
    value_grad = jnp.einsum(
        "shqk,sqhd->skhd",
        probs.astype(jnp.bfloat16),
        out_grad_low,
        preferred_element_type=jnp.float32,
    )
    piece_grad = jnp.stack([key_grad, value_grad], 2).reshape(
        slot_count, per_slot, piece_width, 2 * model_width
    )
    pair_grad = piece_grad
    query_grad, pair_grad = (query_grad, pair_grad)
    own_pair = (
        lax.psum_scatter(pair_grad.astype(jnp.bfloat16), "blk", scatter_dimension=2, tiled=True)
        .astype(jnp.float32)
        .reshape(row_count, 2 * model_width)
    )
    qkv_low = jnp.concatenate(
        [query_grad.reshape(row_count, model_width) * 0.125, own_pair], 1
    ).astype(jnp.bfloat16)
    qkv_weight_grad = left_outer(normed_low, qkv_low)
    input_grad, first_gain_grad, first_shift_grad = first_back(right_outer(qkv_low, qkv_weight))
    tokens_grad = (input_grad + hidden_grad).astype(jnp.bfloat16).reshape(tokens.shape)
    (
        first_gain_grad,
        first_shift_grad,
        qkv_weight_grad,
        proj_weight_grad,
        proj_bias_grad,
        second_gain_grad,
        second_shift_grad,
        expand_weight_grad,
        expand_bias_grad,
        reduce_weight_grad,
        reduce_bias_grad,
        score_gain_grad,
        score_shift_grad,
        score_weight_grad,
        score_bias_grad,
        pred_weight_grad,
        pred_bias_grad,
        mid_weight_grad,
        mid_bias_grad,
        last_weight_grad,
        last_bias_grad,
    ) = lax.psum(
        (
            first_gain_grad,
            first_shift_grad,
            qkv_weight_grad,
            proj_weight_grad,
            proj_bias_grad,
            second_gain_grad,
            second_shift_grad,
            expand_weight_grad,
            expand_bias_grad,
            reduce_weight_grad,
            reduce_bias_grad,
            score_gain_grad,
            score_shift_grad,
            score_weight_grad,
            score_bias_grad,
            pred_weight_grad,
            pred_bias_grad,
            mid_weight_grad,
            mid_bias_grad,
            last_weight_grad,
            last_bias_grad,
        ),
        ("img", "blk"),
    )
    return (
        out_tokens,
        keep_prob,
        tokens_grad,
        first_gain_grad,
        first_shift_grad,
        qkv_weight_grad,
        proj_weight_grad,
        proj_bias_grad,
        second_gain_grad,
        second_shift_grad,
        expand_weight_grad,
        expand_bias_grad,
        reduce_weight_grad,
        reduce_bias_grad,
        score_gain_grad,
        score_shift_grad,
        score_weight_grad,
        score_bias_grad,
        pred_weight_grad,
        pred_bias_grad,
        mid_weight_grad,
        mid_bias_grad,
        last_weight_grad,
        last_bias_grad,
    )


LONGEST = 325
CHUNK = 32
ROWS = 256
BF = jnp.bfloat16
F32 = jnp.float32


def dot(a, b):
    return lax.dot_general(a, b, (((1,), (0,)), ((), ())), preferred_element_type=F32)


def dot_nt(a, b):
    return lax.dot_general(a, b, (((1,), (1,)), ((), ())), preferred_element_type=F32)


def dot_tn(a, b):
    return lax.dot_general(a, b, (((0,), (0,)), ((), ())), preferred_element_type=F32)


def split_two(v):
    high = v.astype(BF)
    return high, (v - high.astype(F32)).astype(BF)


def gelu_pair(v):
    phi = 0.5 * (1.0 + lax.erf(v * math.sqrt(0.5)))
    density = jnp.exp(v * v * -0.5) * (1.0 / math.sqrt(2.0 * math.pi))
    return v * phi, phi + v * density


def normalise(v):
    centre = v - jnp.mean(v, -1, keepdims=True)
    spread = jnp.mean(centre * centre, -1, keepdims=True)
    scale = lax.rsqrt(spread + EPS)
    return centre * scale, scale


def norm_back(grad, unit, scale, gain):
    inner = grad * gain
    mean_one = jnp.mean(inner, -1, keepdims=True)
    mean_two = jnp.mean(inner * unit, -1, keepdims=True)
    return scale * (inner - mean_one - unit * mean_two)


def total_rows(v):
    return jnp.sum(v.astype(F32), 0, keepdims=True)


def lanes(width):
    return lax.broadcasted_iota(jnp.int32, (1, width), 1)


def features(v):
    high = v.astype(BF)
    rest = v - high.astype(F32)
    middle = rest.astype(BF)
    least = (rest - middle.astype(F32)).astype(BF)
    spot = lanes(v.shape[1]) % HEAD
    zero = jnp.zeros_like(high)
    return jnp.where(spot == 0, high, jnp.where(spot == 1, middle, jnp.where(spot == 2, least, zero)))


def window(first, last, length, tile):
    if length < 650:
        return 0, length
    low = 0 if first < LONGEST else max(LONGEST, first - LONGEST + 1)
    high = LONGEST if last <= LONGEST else min(length, last - 1 + LONGEST)
    return low // tile * tile, min(length, -(-high // tile) * tile)


class Place:
    def __init__(self, axis, length, ends):
        self.axis, self.length, self.ends = axis, length, ends
        self.tile = CHUNK * axis

    def places(self, rows):
        return rows // self.tile * self.tile + rows % CHUNK * self.axis + rows % self.tile // CHUNK

    def segments(self, places):
        total = jnp.zeros_like(places)
        for end in self.ends:
            total += (places >= end).astype(jnp.int32)
        return total

    def column(self, start, count):
        rows = start + lax.broadcasted_iota(jnp.int32, (count, 1), 0)
        return self.places(rows)

    def row(self, start, count):
        rows = start + lax.broadcasted_iota(jnp.int32, (1, count), 1)
        return self.places(rows)


VEC = SimpleNamespace(
    first_gain=0, first_shift=1, proj_bias=2, second_gain=3, second_shift=4, expand_bias=5, reduce_bias=9,
    score_gain=10, score_shift=11, score_bias=12, pred_bias=13, mid_bias=14, last_weight=15, last_bias=16,
    query_sum=17, key_sum=18, value_sum=19,
)
VEC_ROWS = 32
MESH = pl.DeviceIdType.MESH
VMEM = pltpu.VMEM
DMA = pltpu.SemaphoreType.DMA


def names_of(**named):
    return tuple(named)


WEIGHTS = names_of(
    first_gain=0, first_shift=0, qkv_weight=0, proj_weight=0, proj_bias=0, second_gain=0, second_shift=0,
    expand_weight=0, expand_bias=0, reduce_weight=0, reduce_bias=0, score_gain=0, score_shift=0, score_weight=0,
    score_bias=0, pred_weight=0, pred_bias=0, mid_weight=0, mid_bias=0, last_weight=0, last_bias=0,
)
LARGE = names_of(
    qkv_weight=0, proj_weight=0, expand_weight=0, reduce_weight=0, score_weight=0, pred_weight=0, mid_weight=0
)
LAST_BIAS = WEIGHTS[-1]
LOADED = LARGE + tuple(n for n in WEIGHTS if n not in LARGE and n != LAST_BIAS)
SUMS = 7
PARTS = 4


class Sizes:
    def __init__(self, axis, groups, width, model, hidden, mid, images):
        self.axis, self.groups, self.width, self.model = axis, groups, width, model
        self.hidden, self.mid, self.images = hidden, mid, images
        self.length = axis * width
        self.tile = CHUNK * axis
        self.tiles = self.length // self.tile
        self.pairs = model // 128
        self.far = groups // 2
        step = 8 * self.far * 16
        self.filled = [0] * SUMS
        wide = model * self.pairs
        self.at = SimpleNamespace(
            score=self.reserve(0, wide), pred=self.reserve(0, model // 2 * self.pairs), mid=self.reserve(0, model // 2),
            reduce=self.reserve(1, hidden * self.pairs), expand=self.reserve(2, model * (hidden // 128)),
            proj=self.reserve(3, wide),
            qkv=[self.reserve(3 + min(p, 2), 3 * model) for p in range(self.pairs)],
            vec=self.reserve(6, VEC_ROWS * self.pairs),
        )
        self.kinds = [BF] * (SUMS - 1) + [F32]
        steps = [step] * (SUMS - 1) + [step // 2]
        self.rows = [-(-rows // each) * each for rows, each in zip(self.filled, steps)]
        self.windows = [window(i, i + ROWS, self.length, self.tile) for i in range(0, self.length, ROWS)]

    def reserve(self, group, rows):
        self.filled[group] += rows
        return group, self.filled[group] - rows


class Links:
    def __init__(self, far, send, receive):
        img, blk = lax.axis_index("img"), lax.axis_index("blk")
        self.far = far
        self.z, self.y, self.x, self.c = img // 2, img % 2, blk // 2, blk % 2
        self.send, self.receive, self.used, self.started = send, receive, 0, []

    def device(self, z, y, x, c):
        return (z * 2 + y, x * 2 + c)

    def mate(self):
        return self.device(self.z, self.y, self.x, 1 - self.c)

    def along(self, turn):
        return self.device(self.z, (self.y + turn) % 2, (self.x + 1 - turn) % 2, self.c)

    def level(self, k):
        return self.device((self.z + k) % self.far, self.y, self.x, self.c)

    def block(self, k):
        x, c = (self.x + k // 2) % 2, (self.c + k % 2) % 2
        return self.device(self.z, self.y, x, c), x * 2 + c

    def copy(self, source, target, device):
        i = self.used
        self.used += 1
        made = pltpu.make_async_remote_copy(
            src_ref=source, dst_ref=target, send_sem=self.send.at[i], recv_sem=self.receive.at[i],
            device_id=device, device_id_type=MESH,
        )
        made.start()
        self.started.append(made)
        return made

    def enter(self, meanwhile):
        barrier = pltpu.get_barrier_semaphore()
        partners = [self.block(k)[0] for k in (1, 2, 3)] + [self.along(1)]
        partners += [self.level(k) for k in range(1, self.far)]
        for partner in partners:
            pl.semaphore_signal(barrier, inc=1, device_id=partner, device_id_type=MESH)
        meanwhile()
        pl.semaphore_wait(barrier, len(partners))

    def finish(self):
        for made in self.started:
            made.wait_send()


def add_rows(target, start, other, other_start, count, step):
    def one(i, _):
        a = pl.ds(pl.multiple_of(start + i * step, 8), step)
        b = pl.ds(pl.multiple_of(other_start + i * step, 8), step)
        target[a, :] = target[a, :] + other[b, :]
        return 0

    lax.fori_loop(0, count // step, one, 0)


class Level:
    def __init__(self, links, turn, flat, deep):
        self.links, self.turn, self.flat = links, turn, flat
        self.deep = links.far if deep else 1
        self.size = flat * self.deep

    def place(self, x, y, z):
        if self.flat == 1:
            at = 0
        elif self.turn is None:
            at = x * 2 + y
        else:
            at = x * (1 - self.turn) + y * self.turn
        return at * self.deep + (z if self.deep > 1 else 0)

    def mine(self):
        return self.place(self.links.x, self.links.y, self.links.z)

    def partner(self, k, back=1):
        t = self.links
        flat, z = k // self.deep, (t.z + back * (k % self.deep) + t.far) % t.far
        if self.flat == 1:
            x, y = t.x, t.y
        elif self.turn is None:
            x, y = (t.x + flat // 2) % 2, (t.y + flat % 2) % 2
        else:
            x, y = (t.x + (1 - self.turn) * flat) % 2, (t.y + self.turn * flat) % 2
        return t.device(z, y, x, t.c), self.place(x, y, z)


def levels_of(links, kind, core):
    both, deep = Level(links, None, 4, False), Level(links, 0, 1, True)
    x, y = Level(links, 0, 2, False), Level(links, 1, 2, False)
    if kind == TURNS:
        return [Level(links, core, 2, False), Level(links, 1 - core, 2, False), deep]
    return {FLAT: [both, deep], Y_FIRST: [y, x, deep], ALL: [Level(links, None, 4, True)], Y_DEEP: [y, deep, x]}[kind]


TURNS, FLAT, Y_FIRST, ALL, Y_DEEP = range(5)


def sum_group(links, kind, rows, buf, out, mate_in, level_in, own, own_sem):
    c = links.c
    levels = levels_of(links, kind, c)
    first_of_mate = levels_of(links, kind, 1 - c)[0]
    mate = links.mate()
    half = rows // 2
    n = half // (4 * links.far)

    def part(ref, start, size):
        return ref.at[pl.ds(pl.multiple_of(start, 8), size), :]

    def ordered(level, core_level):
        k = level.size
        return [core_level.partner(j)[1] for j in range(1, k)] + [core_level.mine()]

    base, size = c * half, half
    cut = levels[0].size if levels[0].size <= 4 else 1
    sub = half // cut
    pending = []
    to_mate = ordered(levels[0], first_of_mate) if cut > 1 else [0]
    for at in to_mate:
        pending.append([(links.copy(part(buf, (1 - c) * half + at * sub, sub), part(mate_in, at * sub, sub), mate), mate_in)])
    where = ordered(levels[0], levels[0]) if cut > 1 else [0]
    recv_at = 0
    for i, level in enumerate(levels):
        yield
        step = size // level.size
        following = levels[i + 1] if i + 1 < len(levels) else None
        split = level.size == 2 and following is not None and following.size == 2
        sent = [[], []] if split else [[]]
        spots = [level.partner(k)[1] for k in range(1, level.size)]

        def send(k):
            device, at = level.partner(k)
            slot = recv_at + (k - 1) * step
            if split:
                half_step = step // 2
                for j, two in enumerate((1 - following.mine(), following.mine())):
                    sent[j].append((links.copy(
                        part(buf, base + at * step + two * half_step, half_step),
                        part(level_in, slot + two * half_step, half_step), device), level_in, slot + two * half_step))
            else:
                sent[0].append((links.copy(part(buf, base + at * step, step), part(level_in, slot, step), device), level_in, slot))

        def take(group, at, count, first_in):
            for made in group:
                made[0].wait_recv()
                start = made[2] if len(made) > 2 else first_in
                add_rows(buf, base + at * count, made[1], start, count, min(count, 8 * n))

        if len(pending) == level.size:
            for k, (group, at) in enumerate(zip(pending, where), 1):
                take(group, at, step, at * step)
                if k < level.size:
                    send(k)
        else:
            for group in pending:
                take(group, 0, size, 0)
            for k in range(1, level.size):
                send(k)
        recv_at += (level.size - 1) * step
        base, size = base + level.mine() * step, step
        pending = sent
        where = [1 - following.mine(), following.mine()] if split else [0]
    yield
    total = buf[pl.ds(pl.multiple_of(base, 8), n), :].astype(F32)
    for made, ref, slot in pending[0]:
        made.wait_recv()
        total += ref[pl.ds(pl.multiple_of(slot, 8), n), :].astype(F32)
    own[...] = total.astype(own.dtype)
    at = part(out, base, n)
    local = pltpu.make_async_copy(own, at, own_sem)
    local.start()
    inner = levels[-1]
    back = [links.copy(own, at, inner.partner(k)[0]) for k in range(1, inner.size)]
    yield
    for made in back:
        made.wait_recv()
    local.wait()
    piece = n * inner.size
    base = base - inner.mine() * n
    outer = levels[:-1]
    flying = [[] for _ in outer]
    to_mate = []

    def pass_on(start, level_count):
        whole = part(out, start, piece)
        for i in reversed(range(level_count)):
            for k in range(1, outer[i].size):
                flying[i].append((k, links.copy(whole, whole, outer[i].partner(k)[0]), start))
        to_mate.append(links.copy(whole, whole, mate))

    pass_on(base, len(outer))
    step = piece
    for i in reversed(range(len(outer))):
        yield
        level = outer[i]
        for k, made, start in list(flying[i]):
            made.wait_recv()
            pass_on(start + (level.partner(k, -1)[1] - level.mine()) * step, i)
        step *= level.size
    yield
    for made in to_mate:
        made.wait_recv()


def layer_kernel(z, names, *refs):
    r = SimpleNamespace(**dict(zip(names, refs)))
    length, model, axis, pairs = z.length, z.model, z.axis, z.pairs
    tile, width = z.tile, z.width
    chunks = z.hidden // model
    links = Links(z.far, r.send, r.receive)
    mine = links.x * 2 + links.c
    local_used = [0]

    def local_copy(source, target):
        i = local_used[0]
        local_used[0] += 1
        made = pltpu.make_async_copy(source, target, r.load.at[i])
        made.start()
        return made

    small_loads = [
        local_copy(source, target)
        for source, target in ((r.keep_in, r.keep_in_v), (r.noise, r.noise_v), (r.grad_keep, r.grad_keep_v))
    ]
    w = SimpleNamespace(**{n: getattr(r, n + VALUE) for n in LOADED})
    given = w
    small_send, small = r.small_send, r.small

    def collect():
        for made in small_loads:
            made.wait()
        for s in range(axis):
            small_send[s, 0:1, :] = r.keep_in_v[s].astype(F32)
            small_send[s, 1:3, :] = r.noise_v[s]
            small_send[s, 3:4, :] = r.grad_keep_v[s]
            small_send[s, 4:8, :] = jnp.zeros((4, width), F32)

    links.enter(collect)

    halves = [slice(h * z.tiles // 2, (h + 1) * z.tiles // 2) for h in range(2)]

    def spread(source, target, part):
        return [
            links.copy(source.at[links.block(k)[1], part], target.at[part, mine], links.block(k)[0]) for k in (2, 3, 1)
        ]

    small_copies = [links.copy(small_send.at[links.block(k)[1]], small.at[mine], links.block(k)[0]) for k in (2, 3, 1)]
    token_copies = [spread(r.tokens, r.tok, part) for part in halves]
    loads = {n: local_copy(getattr(r, n), getattr(r, n + VALUE)) for n in LOADED}
    token_local = local_copy(r.tokens.at[mine], r.tok.at[:, mine])
    grad_local = local_copy(r.grad_out.at[mine], r.gout.at[:, mine])
    small[mine] = small_send[mine]

    ends = []
    total = 0
    for i in range(z.images):
        total = total + r.lengths[mine, i]
        ends.append(total)
    place = Place(axis, length, ends)

    meta, kept_row, vec = r.meta, r.kept_row, r.vec
    vec[...] = jnp.zeros_like(vec)
    groups = [r.buf0, r.buf1, r.buf2, r.buf3, r.buf4, r.buf5, r.buf6]
    for g in range(SUMS):
        if z.filled[g] < z.rows[g]:
            groups[g][z.filled[g] :, :] = jnp.zeros((z.rows[g] - z.filled[g], 128), z.kinds[g])
    for made in small_copies:
        made.wait_recv()
    for p in range(axis):
        block = jnp.concatenate([small[p], jnp.zeros((120, width), F32)], 0).T
        for t in range(z.tiles):
            meta[t * tile + p * CHUNK : t * tile + (p + 1) * CHUNK, :] = block[t * CHUNK : (t + 1) * CHUNK, :]
    for t in range(length // 128):
        kept_row[:, t * 128 : (t + 1) * 128] = meta[t * 128 : (t + 1) * 128, :].T[0:8]

    bias = [r.bias0, r.bias1, r.bias2, r.bias3]
    for i, (low, high) in enumerate(z.windows):
        spot_q, spot_k = place.column(i * ROWS, ROWS), place.row(low, high - low)
        segment_k = jnp.where((kept_row[0:1, low:high] > 0) & (spot_k < ends[-1]), place.segments(spot_k), -1)
        allowed = (place.segments(spot_q) == segment_k) | (spot_q == spot_k)
        bias[i][...] = jnp.where(allowed, 0.0, NEG)

    def vec_set(at, value):
        vec[at : at + 1, : value.shape[1]] = value

    def put(where, value, rows=0):
        group, at = where
        value = value.astype(z.kinds[group])
        for j in range(value.shape[1] // 128):
            groups[group][at + rows : at + rows + value.shape[0], :] = value[:, j * 128 : (j + 1) * 128]
            rows += value.shape[0]

    def row(ref):
        return ref[...].reshape(1, -1)

    def flat(ref):
        return ref[...].reshape(length, model)

    def tiled(ref, value):
        ref[...] = value.reshape(z.tiles, axis, CHUNK, model)

    spot = place.column(0, length)
    segment = place.segments(spot)
    live = (spot < ends[-1]).astype(F32)
    kept = jnp.where(meta[:, 0:1] > 0, live, 0.0)
    member = (segment == lanes(128)).astype(F32)
    r.member[...] = member.astype(BF)
    r.chosen[...] = (member * kept).astype(BF)

    for n in (LARGE[0], WEIGHTS[0], WEIGHTS[1]):
        loads.pop(n).wait()
    for t in (1, 2):
        r.weight_turned[t - 1] = w.qkv_weight[:, t * model : (t + 1) * model].T
    token_local.wait()
    half = lanes(128) < HEAD

    def project(h):
        rows = slice(h * length // 2, (h + 1) * length // 2)
        unit, _s = normalise(r.tok[halves[h]].reshape(length // 2, model).astype(F32))
        r.unit_low[rows, :] = unit.astype(BF)
        low = (unit * row(given.first_gain) + row(given.first_shift)).astype(BF)
        r.query[rows, :] = (dot(low, w.qkv_weight[:, :model]) * 0.125).astype(BF)
        key = dot(low, w.qkv_weight[:, model : 2 * model]).astype(BF)
        value = dot(low, w.qkv_weight[:, 2 * model :]).astype(BF)
        ones = jnp.ones((length // 2, 128), BF)
        for p in range(pairs):
            for ref, kind in ((r.key_ones, key), (r.value_ones, value)):
                ref[rows, p * 256 : p * 256 + 128] = kind[:, p * 128 : (p + 1) * 128]
                ref[rows, p * 256 + 128 : (p + 1) * 256] = ones

    def attend(i):
        low, high = z.windows[i]
        rows = slice(i * ROWS, (i + 1) * ROWS)
        for p in range(pairs):
            at = slice(p * 128, (p + 1) * 128)
            q = r.query[rows, at]
            outs, logs = [], []
            for side in (half, ~half):
                masked = jnp.where(side, q, jnp.zeros_like(q))
                scores = dot_nt(masked, r.key_ones[low:high, p * 256 : p * 256 + 128]) + bias[i][...]
                top = jnp.max(scores, -1, keepdims=True)
                weights = jnp.exp(scores - top).astype(BF)
                both = dot(weights, r.value_ones[low:high, p * 256 : (p + 1) * 256])
                outs.append(both[:, :128] / both[:, 128:])
                logs.append(top + jnp.log(both[:, 128:]))
            r.heads_out[rows, at] = jnp.where(half, outs[0], outs[1])
            r.lse_parts[rows, at] = features(-jnp.where(half, logs[0], logs[1]))

    early = [i for i, (_, high) in enumerate(z.windows) if max(high, (i + 1) * ROWS) <= length // 2]
    for h in range(2):
        for made in token_copies[h]:
            made.wait_recv()
        project(h)
        for i in range(len(z.windows)):
            if (i in early) == (h == 0):
                attend(i)
        if h == 0:
            grad_copies = spread(r.grad_out, r.gout, slice(0, z.tiles))

    for made in loads.values():
        made.wait()

    low = r.heads_out[...].astype(BF)
    r.attended[...] = low
    hid = flat(r.tok).astype(F32) + dot(low, w.proj_weight[...]) + row(given.proj_bias)
    r.hidden[...] = hid
    unit, _s = normalise(hid)
    low = (unit * row(given.second_gain) + row(given.second_shift)).astype(BF)
    r.normed_two[...] = low
    expand_bias = row(given.expand_bias)
    for c in range(chunks):
        at = slice(c * model, (c + 1) * model)
        act, slope = gelu_pair(dot(low, w.expand_weight[:, at]) + expand_bias[:, at])
        r.active[:, at] = act.astype(BF)
        r.expand_low[:, at] = slope.astype(BF)
    blk = hid + dot(r.active[...], w.reduce_weight[...]) + row(given.reduce_bias)
    r.block[...] = blk
    tiled(r.out_v, (blk * live).astype(BF))
    unit, _s = normalise(blk)
    low = (unit * row(given.score_gain) + row(given.score_shift)).astype(BF)
    r.score_in[...] = low
    act, slope = gelu_pair(dot(low, w.score_weight[...]) + row(given.score_bias))
    r.score_act[...] = act
    r.score_slope[...] = slope

    returned, locals_left = [], []

    def give_back(source, target):
        locals_left.append(local_copy(source.at[:, mine], target.at[mine]))
        for k in (2, 3, 1):
            device, at = links.block(k)
            returned.append(links.copy(source.at[:, at], target.at[mine], device))

    give_back(r.out_v, r.out_tokens)

    sums = dot_tn(r.chosen[...], act.astype(BF))
    counts = dot_tn(r.chosen[...], jnp.ones((length, 128), BF))
    inverse = jnp.tile(1.0 / jnp.maximum(counts, 1.0), (1, pairs))
    means = (sums * inverse).astype(BF)
    local_columns = lanes(model) < model // 2
    weight_gap = w.last_weight[0:1, :].astype(F32) - w.last_weight[1:2, :].astype(F32)
    bias_gap = r.last_bias[0] - r.last_bias[1]

    spread_mean = dot(r.member[...], means)
    join = jnp.where(local_columns, r.score_act[...], spread_mean).astype(BF)
    r.joined[...] = join
    act, pred_slope = gelu_pair(dot_nt(join, w.pred_weight[...]) + row(given.pred_bias))
    pred_low = act.astype(BF)
    r.pred_act[...] = pred_low
    act, mid_slope = gelu_pair(dot(pred_low, w.mid_weight[...]) + row(given.mid_bias))
    mid_low = act.astype(BF).astype(F32)
    info = meta[...]
    margin = jnp.sum(mid_low * weight_gap, -1, keepdims=True) + bias_gap + info[:, 1:2] - info[:, 2:3]
    sig = 1.0 / (1.0 + jnp.exp(-margin))
    r.keep_col[...] = jnp.broadcast_to(sig * kept, (length, 128))
    margin_grad = info[:, 3:4] * kept * sig * (1.0 - sig)
    vec_set(VEC.last_weight, jnp.sum(mid_low * margin_grad, 0, keepdims=True))
    vec_set(VEC.last_bias, jnp.sum(jnp.broadcast_to(margin_grad, (length, 128)), 0, keepdims=True))
    mid_grad = (margin_grad * weight_gap * mid_slope).astype(BF)
    r.mid_grad_low[...] = mid_grad
    vec_set(VEC.mid_bias, total_rows(mid_grad))
    pred_grad = (dot_nt(mid_grad, w.mid_weight[...]) * pred_slope).astype(BF)
    r.pred_grad_low[...] = pred_grad
    vec_set(VEC.pred_bias, total_rows(pred_grad))
    join_grad = dot(pred_grad, w.pred_weight[...])
    r.score_act[...] = join_grad
    mean_grad = (dot_tn(r.member[...], join_grad.astype(BF)) * inverse).astype(BF)

    def summing(g, names):
        return sum_group(links, KINDS[g], z.rows[g], *[getattr(r, n + str(g)) for n in names], r.own_sem.at[g])

    sum_names = names_of(buf=0, sum=0, mate_in=0, level_in=0, own=0)
    running = [summing(g, sum_names) for g in range(SUMS)]

    def advance(*which):
        for g in which:
            next(running[g], None)

    def point(i):
        advance(*PLAN.get(i, ()))

    spread_grad = dot(r.chosen[...], mean_grad)
    low = (jnp.where(local_columns, r.score_act[...], spread_grad) * r.score_slope[...]).astype(BF)
    r.score_grad_low[...] = low
    vec_set(VEC.score_bias, total_rows(low))
    grad_local.wait()
    for made in grad_copies:
        made.wait_recv()
    grad = dot_nt(r.score_grad_low[...], w.score_weight[...])
    unit, scale = normalise(r.block[...])
    vec_set(VEC.score_gain, jnp.sum(grad * unit, 0, keepdims=True))
    vec_set(VEC.score_shift, jnp.sum(grad, 0, keepdims=True))
    blk_grad = norm_back(grad, unit, scale, row(given.score_gain)) + flat(r.gout).astype(F32) * live
    r.block[...] = blk_grad
    low = blk_grad.astype(BF)
    r.block_low[...] = low
    vec_set(VEC.reduce_bias, total_rows(low))
    point(0)
    for c in range(chunks):
        part = dot_tn(r.active[:, c * model : (c + 1) * model], r.block_low[...]).astype(BF)
        for j in range(pairs):
            put(z.at.reduce, part[:, j * 128 : (j + 1) * 128], j * z.hidden + c * model)
        point(30 + c)
    advance(1)
    point(1)
    for c in range(chunks):
        at = slice(c * model, (c + 1) * model)
        piece = (dot_nt(r.block_low[...], w.reduce_weight[at, :]) * r.expand_low[:, at].astype(F32)).astype(BF)
        r.expand_low[:, at] = piece
        vec_set(VEC.expand_bias + c, total_rows(piece))
        put(z.at.expand, dot_tn(r.normed_two[...], piece), c * pairs * model)
        if c + 1 == chunks:
            advance(2)
        point(2 + c)

    put(z.at.score, dot_tn(r.score_in[...], r.score_grad_low[...]))
    put(z.at.pred, dot_tn(r.pred_grad_low[...], r.joined[...]))
    mid = dot_tn(r.pred_act[...], r.mid_grad_low[...])
    put(z.at.mid, jnp.concatenate([mid, jnp.zeros((model // 2, 128 - z.mid), F32)], 1))
    advance(0)

    for p in range(axis):
        parts = [r.keep_col[t * tile + p * CHUNK : t * tile + (p + 1) * CHUNK, :] for t in range(z.tiles)]
        r.keep_v[p] = jnp.concatenate(parts, 0).T[0:8]
    for k in (2, 3, 1):
        device, at = links.block(k)
        returned.append(links.copy(r.keep_v.at[at], r.keep.at[mine], device))
    locals_left.append(local_copy(r.keep_v.at[mine], r.keep.at[mine]))

    grad = dot_nt(r.expand_low[...], w.expand_weight[...])
    unit, scale = normalise(r.hidden[...])
    vec_set(VEC.second_gain, jnp.sum(grad * unit, 0, keepdims=True))
    vec_set(VEC.second_shift, jnp.sum(grad, 0, keepdims=True))
    hid_grad = norm_back(grad, unit, scale, row(given.second_gain)) + r.block[...]
    r.hidden[...] = hid_grad
    low = hid_grad.astype(BF)
    r.hidden_low[...] = low
    vec_set(VEC.proj_bias, total_rows(low))
    point(40)
    low = dot_nt(low, w.proj_weight[...]).astype(BF)
    r.attended_grad[...] = low
    one, two = split_two(low.astype(F32) * r.heads_out[...])
    pair_sum = (
        lax.broadcasted_iota(jnp.int32, (128, 128), 0) // HEAD == lax.broadcasted_iota(jnp.int32, (128, 128), 1) // HEAD
    ).astype(BF)
    for p in range(pairs):
        at = slice(p * 128, (p + 1) * 128)
        r.delta_parts[:, at] = features(-(dot(one[:, at], pair_sum) + dot(two[:, at], pair_sum)))
    r.query_turned[...] = r.query[...].T
    point(6)
    put(z.at.proj, dot_tn(r.attended[...], r.hidden_low[...]))
    point(7)
    r.attended_turned[...] = r.attended_grad[...].T

    r.key_turned[...] = jnp.zeros((model, length), F32)
    r.value_turned[...] = jnp.zeros((model, length), F32)
    unit_count = 0
    for p in range(pairs):
        at = slice(p * 128, (p + 1) * 128)
        wide = slice(p * 256, (p + 1) * 256)
        near = slice(p * 256, p * 256 + 128)
        for i, (low, high) in enumerate(z.windows):
            rows = slice(i * ROWS, (i + 1) * ROWS)
            q, lse, og, delta = r.query[rows, at], r.lse_parts[rows, at], r.attended_grad[rows, at], r.delta_parts[rows, at]
            zero = jnp.zeros_like(q)
            query_parts = []
            for h, side in enumerate((half, ~half)):
                head = slice((2 * p + h) * HEAD, (2 * p + h + 1) * HEAD)
                wide_q = jnp.concatenate([jnp.where(side, q, zero), jnp.where(side, lse, zero)], 1)
                wide_o = jnp.concatenate([jnp.where(side, og, zero), jnp.where(side, delta, zero)], 1)
                probs = jnp.exp(dot_nt(wide_q, r.key_ones[low:high, wide]) + bias[i][...])
                score_grad = (probs * dot_nt(wide_o, r.value_ones[low:high, wide])).astype(BF)
                r.value_turned[head, low:high] += dot(r.attended_turned[head, rows], probs.astype(BF))
                r.key_turned[head, low:high] += dot(r.query_turned[head, rows], score_grad)
                query_parts.append(dot(score_grad, r.key_ones[low:high, near]))
            r.query_grad[rows, at] = (jnp.where(half, query_parts[0], query_parts[1]) * 0.125).astype(BF)
            point(8 + unit_count)
            unit_count += 1
        part = r.query_grad[:, at]
        put(z.at.qkv[p], dot_tn(r.unit_low[...], part))
        vec[VEC.query_sum : VEC.query_sum + 1, at] = total_rows(part)
        for t, (ref, name) in enumerate(((r.key_turned, VEC.key_sum), (r.value_turned, VEC.value_sum)), 1):
            part = ref[at, :].astype(BF)
            r.turned_low[t - 1, at, :] = part
            put(z.at.qkv[p], dot(part, r.unit_low[...]), t * model)
            vec[name : name + 1, at] = dot_nt(jnp.ones((8, length), BF), part)[0:1]
        advance(z.at.qkv[p][0])
    put(z.at.vec, vec[...])
    advance(6)
    point(20)

    grad = dot_nt(r.query_grad[...], w.qkv_weight[:, :model])
    for t in range(2):
        grad += dot_tn(r.turned_low[t], r.weight_turned[t])
    point(41)
    unit, scale = normalise(flat(r.tok).astype(F32))
    tiled(r.grad_v, (norm_back(grad, unit, scale, row(given.first_gain)) + r.hidden[...]).astype(BF))
    locals_left.append(local_copy(r.grad_v.at[:, mine], r.tokens_grad.at[mine]))

    def give_part(i):
        part = slice(i * z.tiles // PARTS, (i + 1) * z.tiles // PARTS)
        for k in (2, 3, 1):
            device, at = links.block(k)
            returned.append(links.copy(r.grad_v.at[part, at], r.tokens_grad.at[mine, part], device))

    point(21)
    given_parts = 0
    for g in PLAN_END + (SUMS,) * PARTS:
        if g < SUMS:
            advance(g)
        elif given_parts < PARTS:
            give_part(given_parts)
            given_parts += 1
    for _ in range(20):
        advance(*range(SUMS))
    for made in returned:
        made.wait_recv()
    for made in locals_left:
        made.wait()
    links.finish()


VALUE = "_v"
KINDS = (FLAT, TURNS, TURNS, TURNS, TURNS, TURNS, FLAT)
PLAN = {5: (1,), 40: (0,), 7: (2,), 10: (1,), 13: (3,), 14: (2,), 15: (1,), 16: (0,), 17: (3,), 19: (2, 4), 41: (6, 3, 5, 1)}
PLAN_END = (4, 0, 7, 5, 7, 7, 6, 4, 3, 5, 2, 1, 6, 0, 3, 5, 1, 4, 2, 3, 5, 1, 6, 4, 2, 5, 4, 1, 3, 6, 7, 3, 2, 5, 0, 4, 6, 5, 2, 0, 4)


def run_layer(z, tokens, grad_out, keep_in, noise, grad_keep, lengths, weights):
    L, D, U = z.length, z.model, z.hidden
    half = D // 2
    sm, far = (pl.BlockSpec(memory_space=m) for m in (pltpu.SMEM, pl.ANY))
    inputs = dict(
        tokens=(tokens, far), grad_out=(grad_out, far), keep_in=(keep_in, far), noise=(noise, far),
        grad_keep=(grad_keep, far), lengths=(lengths, sm),
    )
    for n in WEIGHTS:
        inputs[n] = (weights[n], sm if n == LAST_BIAS else far)
    four = jax.ShapeDtypeStruct((z.axis, z.tiles, CHUNK, D), BF)
    outs = dict(out_tokens=four, keep=jax.ShapeDtypeStruct((z.axis, 8, z.width), F32), tokens_grad=four)
    low = lambda *s: VMEM(s, BF)
    full = lambda *s: VMEM(s, F32)
    tiles = low(z.tiles, z.axis, CHUNK, D)
    small = full(z.axis, 8, z.width)
    scratch = dict(
        tok=tiles, gout=tiles, out_v=tiles, grad_v=tiles, small_send=small, small=small, keep_v=small,
        meta=full(L, 128), kept_row=full(8, L), member=low(L, 128), chosen=low(L, 128),
        unit_low=low(L, D), query=low(L, D), query_turned=low(D, L), attended_turned=low(D, L), key_turned=full(D, L),
        value_turned=full(D, L), turned_low=low(2, D, L), weight_turned=low(2, D, D), key_ones=low(L, 2 * D), value_ones=low(L, 2 * D),
        heads_out=full(L, D), lse_parts=low(L, D), delta_parts=low(L, D), attended=low(L, D),
        hidden=full(L, D), normed_two=low(L, D), active=low(L, U), expand_low=low(L, U),
        block=full(L, D), score_in=low(L, D), score_act=full(L, D), score_slope=full(L, D),
        joined=low(L, D), pred_act=low(L, half), mid_grad_low=low(L, z.mid), pred_grad_low=low(L, half),
        score_grad_low=low(L, D), block_low=low(L, D), hidden_low=low(L, D), attended_grad=low(L, D),
        query_grad=low(L, D), vec=full(VEC_ROWS, D), keep_col=full(L, 128),
    )
    for n in LOADED:
        scratch[n + VALUE] = VMEM(weights[n].shape, weights[n].dtype)
    scratch.update(keep_in_v=VMEM(keep_in.shape, jnp.int32), noise_v=full(*noise.shape), grad_keep_v=full(*grad_keep.shape))
    for i, (first, last) in enumerate(z.windows):
        scratch["bias%d" % i] = full(ROWS, last - first)
    sum_names = names_of(sum=0, buf=0, mate_in=0, level_in=0, own=0)
    for g, (rows, kind) in enumerate(zip(z.rows, z.kinds)):
        n = rows // (8 * z.far)
        shapes = [(rows, 128), (rows, 128), (rows // 2, 128), (rows // 2 - n, 128), (n, 128)]
        outs[sum_names[0] + str(g)] = jax.ShapeDtypeStruct(shapes[0], kind)
        scratch.update((name + str(g), VMEM(shape, kind)) for name, shape in zip(sum_names[1:], shapes[1:]))
    sems = 12 + 3 * PARTS + SUMS * 36
    scratch.update(send=DMA((sems,)), receive=DMA((sems,)), load=DMA((len(LOADED) + 8,)), own_sem=DMA((SUMS,)))
    results = pl.pallas_call(
        functools.partial(layer_kernel, z, tuple(inputs) + tuple(outs) + tuple(scratch)),
        out_shape=list(outs.values()),
        in_specs=[spec for _, spec in inputs.values()],
        out_specs=[far] * len(outs),
        scratch_shapes=list(scratch.values()),
        compiler_params=pltpu.CompilerParams(collective_id=0, has_side_effects=True, vmem_limit_bytes=63 * 2**20),
        name="layer",
    )(*[array for array, _ in inputs.values()])
    return dict(zip(outs, results))


STAGED = names_of(reduce_weight=0, score_weight=0, pred_weight=0, expand_weight=0, proj_weight=0, qkv_weight=0)
GIVEN = names_of(qkv_given=0, gain_given=0, shift_given=0)
PASSED = names_of(out_tokens=0, tokens_grad=0)


def unpack_kernel(z, names, *refs):
    r = SimpleNamespace(**dict(zip(names, refs)))
    out = SimpleNamespace(**{n: getattr(r, n + VALUE) if n in STAGED else getattr(r, n) for n in WEIGHTS})
    sums = [r.in0, r.in1, r.in2, r.in3, r.in4, r.in5, r.in6]
    used = [0]

    def start(source, target):
        made = pltpu.make_async_copy(source, target, r.sem.at[used[0]])
        used[0] += 1
        made.start()
        return made

    given = [start(r.qkv_given, r.weight), start(r.gain_given, r.gain), start(r.shift_given, r.shift)]
    loads = [start(source, ref) for source, ref in zip((r.sum0, r.sum1, r.sum2, r.sum3, r.sum4, r.sum5, r.sum6), sums)]
    through = [start(r.out_tokens, r.out_tokens_v), start(r.tokens_grad, r.tokens_grad_v)]
    stored = []
    model, pairs, half = z.model, z.pairs, z.model // 2

    def take(where, first, count):
        group, at = where
        return sums[group][at + first : at + first + count, :].astype(F32)

    def store(*names):
        stored.extend(start(getattr(r, n + VALUE), getattr(r, n)) for n in names)

    loads[0].wait()
    for j in range(pairs):
        at = slice(j * 128, (j + 1) * 128)
        out.score_weight[:, at] = take(z.at.score, j * model, model)
        out.pred_weight[:, at] = take(z.at.pred, j * half, half)
    out.mid_weight[...] = take(z.at.mid, 0, half)[:, : z.mid]
    store(STAGED[1], STAGED[2])
    loads[1].wait()
    for j in range(pairs):
        out.reduce_weight[:, j * 128 : (j + 1) * 128] = take(z.at.reduce, j * z.hidden, z.hidden)
    store(STAGED[0])
    loads[2].wait()
    for j in range(z.hidden // 128):
        out.expand_weight[:, j * 128 : (j + 1) * 128] = take(z.at.expand, j * model, model)
    store(STAGED[3])
    through[0].wait()
    through[1].wait()
    stored.append(start(r.out_tokens_v, r.out_tokens_out))
    stored.append(start(r.tokens_grad_v, r.tokens_grad_out))
    loads[3].wait()
    loads[4].wait()
    loads[5].wait()
    loads[6].wait()
    vec = jnp.concatenate([take(z.at.vec, j * VEC_ROWS, VEC_ROWS) for j in range(pairs)], 1)

    def row(at):
        return vec[at : at + 1, :]

    def turned(ref):
        return jnp.broadcast_to(ref[...].reshape(1, model), (128, model)).T

    for made in given:
        made.wait()
    gain, shift = turned(r.gain), turned(r.shift)
    gain_grad, shift_grad = jnp.zeros((model, 128), F32), jnp.zeros((model, 128), F32)
    for j in range(pairs):
        out.proj_weight[:, j * 128 : (j + 1) * 128] = take(z.at.proj, j * model, model)
        for t, name in enumerate((VEC.query_sum, VEC.key_sum, VEC.value_sum)):
            part = take(z.at.qkv[j], t * model, model)
            if t:
                part = jnp.concatenate([part[b * 128 : (b + 1) * 128, :].T for b in range(pairs)], 0)
            at = slice(t * model + j * 128, t * model + (j + 1) * 128)
            total = row(name)[:, j * 128 : (j + 1) * 128]
            weight = r.weight[:, at].astype(F32)
            out.qkv_weight[:, at] = gain * part + shift * total
            gain_grad += weight * part
            shift_grad += weight * total
    store(STAGED[4], STAGED[5])
    out.first_gain[...] = jnp.sum(gain_grad.T, 0, keepdims=True).reshape(model)
    out.first_shift[...] = jnp.sum(shift_grad.T, 0, keepdims=True).reshape(model)
    chunks = z.hidden // model
    for ref, at in (
        (out.proj_bias, VEC.proj_bias),
        (out.second_gain, VEC.second_gain), (out.second_shift, VEC.second_shift), (out.reduce_bias, VEC.reduce_bias),
        (out.score_gain, VEC.score_gain), (out.score_shift, VEC.score_shift), (out.score_bias, VEC.score_bias),
    ):
        ref[...] = row(at).reshape(model)
    out.expand_bias[...] = jnp.concatenate([row(VEC.expand_bias + c) for c in range(chunks)], 1).reshape(z.hidden)
    out.pred_bias[...] = row(VEC.pred_bias)[:, :half].reshape(half)
    out.mid_bias[...] = row(VEC.mid_bias)[:, : z.mid].reshape(z.mid)
    gap = row(VEC.last_weight)[:, : z.mid]
    out.last_weight[...] = jnp.concatenate([gap, -gap], 0)
    gap = row(VEC.last_bias)[:, 0:2]
    out.last_bias[...] = jnp.where(lanes(2) == 0, gap, -gap).reshape(2)
    for s in range(z.axis):
        r.keep_out[s] = r.keep[s, 0:1, :]
    for made in stored:
        made.wait()


def run_unpack(z, results, shapes, given):
    far, vm = pl.BlockSpec(memory_space=pl.ANY), pl.BlockSpec(memory_space=pltpu.VMEM)
    tokens = results[PASSED[0]]
    outs = dict(
        out_tokens_out=(tokens, far), keep_out=(jax.ShapeDtypeStruct((z.axis, 1, z.width), F32), vm),
        tokens_grad_out=(tokens, far),
    )
    for n in WEIGHTS:
        outs[n] = (jax.ShapeDtypeStruct(shapes[n], F32), far if n in STAGED else vm)
    scratch = dict(out_tokens_v=VMEM(tokens.shape, BF), tokens_grad_v=VMEM(tokens.shape, BF))
    for g in range(SUMS):
        scratch["in%d" % g] = VMEM((z.rows[g], 128), z.kinds[g])
    for n in STAGED:
        scratch[n + VALUE] = VMEM(shapes[n], F32)
    scratch.update(
        sem=DMA((SUMS + 7 + len(STAGED),)), weight=VMEM(given[0].shape, BF), gain=VMEM(given[1].shape, F32),
        shift=VMEM(given[2].shape, F32),
    )
    done = pl.pallas_call(
        functools.partial(unpack_kernel, z, tuple(results) + GIVEN + tuple(outs) + tuple(scratch)),
        out_shape=[jax.ShapeDtypeStruct(s.shape, s.dtype) for s, _ in outs.values()],
        in_specs=[far, vm] + [far] * (SUMS + 4),
        out_specs=[spec for _, spec in outs.values()],
        scratch_shapes=list(scratch.values()),
        compiler_params=pltpu.CompilerParams(vmem_limit_bytes=63 * 2**20),
        name="unpack",
    )(*results.values(), *given)
    return done


def per_device(tokens, lengths, keep_in, noise, *rest):
    weights, (grad_out, grad_keep) = dict(zip(WEIGHTS, rest[:21])), rest[21:]
    slots, width, _, model = tokens.shape
    w = SimpleNamespace(**weights)
    z = Sizes(
        slots, lax.axis_size("img"), width, model, w.expand_weight.shape[1], w.mid_weight.shape[1], lengths.shape[1]
    )
    turned = names_of(pred_weight=0, last_weight=0)
    for n in turned:
        weights[n] = weights[n].T
    four = (slots, width // CHUNK, CHUNK, model)
    results = run_layer(
        z, tokens.reshape(four), grad_out.reshape(four), keep_in.reshape(slots, 1, width),
        noise.reshape(slots, width, 2).swapaxes(1, 2), grad_keep.reshape(slots, 1, width), lengths, weights,
    )
    given = (w.qkv_weight, w.first_gain, w.first_shift)
    done = run_unpack(z, results, {n: v.shape for n, v in weights.items()}, given)
    back = dict(zip(WEIGHTS, done[3:]))
    for n in turned:
        back[n] = back[n].T
    return (
        done[0].reshape(tokens.shape), done[1].reshape(keep_in.shape), done[2].reshape(tokens.shape)
    ) + tuple(back.values())


def solution(mesh):
    split = P("img", None, "blk", None)
    placed = (split, P("img", None), P("img", None, "blk"), split) + (P(),) * 21 + (split, P("img", None, "blk"))

    def chosen_device(*arrays):
        return (per_device if arrays[0].shape[0] == mesh.shape["blk"] == 4 else general_device)(*arrays)

    return jax.shard_map(
        chosen_device, mesh=mesh, in_specs=placed, out_specs=(split, P("img", None, "blk"), split) + (P(),) * 21,
        check_vma=False,
    )
```
